32 devices in a mesh: row: 4 (over x, core), col: 8 (over z, y).
Axes of the slice: x: 2, y: 2, z: 4, core: 2. Of those that a mesh axis runs over, the one named last changes fastest.
Arguments:
- inputs: bfloat16 [256, 8192], P('col', 'row'), may hold values from -1.5 to 1.5
- grad_out: bfloat16 [256, 8192], P('col', 'row'), may hold values from -3 to 3
- gate: bfloat16 [256, 30720], P('row', 'col'), may hold values from -6 to 6
- up: bfloat16 [256, 30720], P('row', 'col'), may hold values from -6 to 6
- gate_weight: bfloat16 [8192, 30720], P('row', 'col'), may hold values from -0.0625 to 0.0625
- up_weight: bfloat16 [8192, 30720], P('row', 'col'), may hold values from -0.0625 to 0.0625
- down_weight: bfloat16 [30720, 8192], P('col', 'row'), may hold values from -0.03125 to 0.03125
Outputs:
- grad_inputs: bfloat16 [256, 8192], P('col', 'row')
- grad_gate_weight: bfloat16 [8192, 30720], P('row', 'col')
- grad_up_weight: bfloat16 [8192, 30720], P('row', 'col')
- grad_down_weight: bfloat16 [30720, 8192], P('col', 'row')
The draws below stay inside these ranges and needn't reach their ends.
All inputs are finite; a program needn't handle non-finite values.
Results may differ from the reference program's by a relative error of at most 0.022.
Values may be sent and summed in bfloat16 or wider, within the bound.
No kernel may reach another device: no remote copies, remote signals or barrier semaphores. Data moves between devices by JAX's collectives and lax.ppermute only.
A program may use at most 192 MiB of HBM per device.

```python
import jax
import jax.numpy as jnp

D = 8192
FF = 30720
TOKENS = 256


def levels(stream_key, dims, split, smallest, high):
    def one(dim, parts):
        steps = jax.random.uniform(jax.random.fold_in(jax.random.fold_in(stream_key, 6), dim), (parts,), jnp.float32, smallest / len(split), high / len(split))
        return jnp.repeat(jnp.exp(steps), dims[dim] // parts).reshape((-1,) + (1,) * (len(dims) - dim - 1))

    level = one(*split[0])
    for cut in split[1:]:
        level = level * one(*cut)
    return level


def bell_draw(key, dims, width, reach, pieces=(), dtype=jnp.bfloat16):
    entries = width * jax.random.normal(key, dims, jnp.float32)
    if pieces:
        entries = entries * levels(key, dims, pieces, -0.22, 0.18)
    return jnp.clip(entries, -reach, reach).astype(dtype)


def setup_inputs(seed: int = 0) -> dict:
    key_list = jax.random.split(jax.random.key(seed), 8)
    inputs = bell_draw(key_list[0], (TOKENS, D), 0.25, 1.5, ((0, 8), (1, 4)))
    grad_out = bell_draw(key_list[1], (TOKENS, D), 0.5, 3.0, ((0, 8), (1, 4)))
    gate = bell_draw(key_list[2], (TOKENS, FF), 1.0, 6.0, ((0, 4), (1, 8)))
    up = bell_draw(key_list[3], (TOKENS, FF), 1.0, 6.0, ((0, 4), (1, 8)))
    gate_weight = bell_draw(key_list[4], (D, FF), D ** -0.5, 0.0625, ((0, 4), (1, 8)))
    up_weight = bell_draw(key_list[5], (D, FF), D ** -0.5, 0.0625, ((0, 4), (1, 8)))
    down_weight = bell_draw(key_list[6], (FF, D), FF ** -0.5, 0.03125, ((0, 8), (1, 4)))
    return dict(inputs=inputs, grad_out=grad_out, gate=gate, up=up, gate_weight=gate_weight, up_weight=up_weight, down_weight=down_weight)


def reference(inputs, grad_out, gate, up, gate_weight, up_weight, down_weight):
    gate_vals = gate.astype(jnp.float32)
    up_vals = up.astype(jnp.float32)
    grad_hidden = jnp.dot(grad_out, down_weight.T, preferred_element_type=jnp.float32)
    sigmoid_gate = jax.nn.sigmoid(gate_vals)
    activated = gate_vals * sigmoid_gate
    grad_gate = (grad_hidden * up_vals * sigmoid_gate * (1.0 + gate_vals * (1.0 - sigmoid_gate))).astype(jnp.bfloat16)
    grad_up = (grad_hidden * activated).astype(jnp.bfloat16)
    hidden = (activated * up_vals).astype(jnp.bfloat16)
    grad_inputs = (jnp.dot(grad_gate, gate_weight.T, preferred_element_type=jnp.float32)
                   + jnp.dot(grad_up, up_weight.T, preferred_element_type=jnp.float32)).astype(jnp.bfloat16)
    grad_gate_weight = jnp.dot(inputs.T, grad_gate, preferred_element_type=jnp.float32).astype(jnp.bfloat16)
    grad_up_weight = jnp.dot(inputs.T, grad_up, preferred_element_type=jnp.float32).astype(jnp.bfloat16)
    grad_down_weight = jnp.dot(hidden.T, grad_out, preferred_element_type=jnp.float32).astype(jnp.bfloat16)
    return grad_inputs, grad_gate_weight, grad_up_weight, grad_down_weight
```

```python
import functools

import jax
import jax.numpy as jnp
from jax import lax
from jax.experimental import pallas as pl
from jax.experimental.pallas import tpu as pltpu
from jax.sharding import PartitionSpec as P

F32 = jnp.float32
BF16 = jnp.bfloat16
CORES = 2
VMEM = 40 * 2**20
NT = (((1,), (1,)), ((), ()))
TN = (((0,), (0,)), ((), ()))


def divisor(size, target, step=128):
    best = size
    for cand in range(step, target + 1, step):
        if size % cand == 0:
            best = cand
    return best


def params(semantics=("arbitrary",)):
    return pltpu.CompilerParams(dimension_semantics=semantics, vmem_limit_bytes=VMEM)


def cost(flops, nbytes):
    return pl.CostEstimate(flops=int(flops), bytes_accessed=int(nbytes), transcendentals=0)


def assemble(blocks, offsets):
    rows, width = blocks[0].shape
    count = len(blocks)

    def kernel(offs, *refs):
        out = refs[count]
        for i in range(count):
            out[pl.ds(pl.multiple_of(offs[i], rows), rows), :] = refs[i][...]

    full = pl.BlockSpec(memory_space=pltpu.VMEM)
    return pl.pallas_call(
        kernel,
        out_shape=jax.ShapeDtypeStruct((rows * count, width), BF16),
        in_specs=[pl.BlockSpec(memory_space=pltpu.SMEM)] + [full] * count,
        out_specs=full,
        compiler_params=pltpu.CompilerParams(vmem_limit_bytes=VMEM),
        cost_estimate=cost(0, 4 * rows * count * width),
        name="assemble",
    )(offsets, *blocks)


def partial_hidden(out_all, down, chunk, chunks):
    tokens, width = out_all.shape
    units = down.shape[0] // chunks
    half = tokens // CORES
    block = divisor(units, 640)
    steps = units // block

    def kernel(a, w, keep, send):
        part = lax.dot_general(a[...], w[...], NT, preferred_element_type=F32).astype(BF16)
        keep[...] = part[:half]
        send[...] = part[half:]

    shape = jax.ShapeDtypeStruct((half, units), BF16)
    return pl.pallas_call(
        kernel,
        grid=(steps,),
        out_shape=(shape, shape),
        in_specs=[
            pl.BlockSpec((tokens, width), lambda i: (0, 0)),
            pl.BlockSpec((block, width), lambda i: (chunk * steps + i, 0)),
        ],
        out_specs=[pl.BlockSpec((half, block), lambda i: (0, i))] * 2,
        compiler_params=params(),
        cost_estimate=cost(2 * tokens * units * width, 2 * units * width + 4 * tokens * units),
        name="partial_hidden",
    )(out_all, down)


def activations(gates, ups):
    count = len(gates)
    rows, width = gates[0].shape
    block = divisor(width, 768)

    def kernel(*refs):
        out = refs[2 * count]
        for i in range(count):
            gate = refs[i][...].astype(F32)
            up = refs[count + i][...].astype(F32)
            out[i * rows : (i + 1) * rows, :] = (gate * jax.nn.sigmoid(gate) * up).astype(BF16)

    return pl.pallas_call(
        kernel,
        grid=(width // block,),
        out_shape=jax.ShapeDtypeStruct((rows * count, width), BF16),
        in_specs=[pl.BlockSpec((rows, block), lambda i: (0, i))] * (2 * count),
        out_specs=pl.BlockSpec((rows * count, block), lambda i: (0, i)),
        compiler_params=params(),
        cost_estimate=cost(10 * rows * count * width, 6 * rows * count * width),
        name="activations",
    )(*gates, *ups)


def hidden_grads(sums, gates, ups, chunk):
    count = len(gates)
    rows = gates[0].shape[0]
    units = sums[0].shape[1]
    block = divisor(units, 640)
    steps = units // block

    def kernel(*refs):
        out = refs[3 * count]
        for i in range(count):
            grad = 0.0
            for o in range(count):
                j = (i - o) % count
                grad = grad + refs[o][j * rows : (j + 1) * rows, :].astype(F32)
            gate = refs[count + i][...].astype(F32)
            up = refs[2 * count + i][...].astype(F32)
            sig = jax.nn.sigmoid(gate)
            at = slice(i * rows, (i + 1) * rows)
            out[0, at, :] = (grad * up * sig * (1.0 + gate * (1.0 - sig))).astype(BF16)
            out[1, at, :] = (grad * gate * sig).astype(BF16)

    return pl.pallas_call(
        kernel,
        grid=(steps,),
        out_shape=jax.ShapeDtypeStruct((2, rows * count, units), BF16),
        in_specs=[pl.BlockSpec((rows * count, block), lambda i: (0, i))] * count
        + [pl.BlockSpec((rows, block), lambda i: (0, chunk * steps + i))] * (2 * count),
        out_specs=pl.BlockSpec((2, rows * count, block), lambda i: (0, 0, i)),
        compiler_params=params(),
        cost_estimate=cost(20 * rows * count * units, 12 * rows * count * units),
        name="hidden_grads",
    )(*sums, *gates, *ups)


def down_grad(mine, other, out_all):
    half, units = mine.shape
    tokens, width = out_all.shape
    block = divisor(units, 384)

    def kernel(a, b, g, out):
        hidden = jnp.concatenate([a[...], b[...]], axis=0)
        out[...] = lax.dot_general(hidden, g[...], TN, preferred_element_type=F32).astype(BF16)

    return pl.pallas_call(
        kernel,
        grid=(units // block,),
        out_shape=jax.ShapeDtypeStruct((units, width), BF16),
        in_specs=[pl.BlockSpec((half, block), lambda i: (0, i))] * 2
        + [pl.BlockSpec((tokens, width), lambda i: (0, 0))],
        out_specs=pl.BlockSpec((block, width), lambda i: (i, 0)),
        compiler_params=params(),
        cost_estimate=cost(2 * tokens * units * width, 2 * units * width),
        name="down_grad",
    )(mine, other, out_all)


def input_grads(mine, other, gate_weight, up_weight, before, offsets, chunk, rows):
    _, half, units = mine.shape
    tokens = 2 * half
    width = gate_weight.shape[0]
    block = divisor(width, 512)
    last = offsets is not None
    count = tokens // rows
    operands, specs = [], []
    if last:
        operands.append(offsets)
        specs.append(pl.BlockSpec(memory_space=pltpu.SMEM))
    operands += [mine, other, gate_weight, up_weight]
    specs += [pl.BlockSpec((2, half, units), lambda i: (0, 0, 0))] * 2
    specs += [pl.BlockSpec((block, units), lambda i: (i, chunk))] * 2
    if before is not None:
        operands.append(before)
        specs.append(pl.BlockSpec((tokens, block), lambda i: (0, i)))

    def kernel(*refs):
        refs = list(refs)
        offs = refs.pop(0) if last else None
        a, b, gw, uw = refs[:4]
        refs = refs[4:]
        total = refs.pop(0)[...] if before is not None else 0.0
        for i, w in enumerate((gw, uw)):
            grads = jnp.concatenate([a[i], b[i]], axis=0)
            total = total + lax.dot_general(grads, w[...], NT, preferred_element_type=F32)
        if not last:
            refs[0][...] = total
            return
        scratch = refs[count]
        scratch[...] = total
        for m in range(count):
            refs[m][...] = scratch[pl.ds(pl.multiple_of(offs[m], rows), rows), :].astype(BF16)

    if last:
        out_shape = [jax.ShapeDtypeStruct((rows, width), BF16)] * count
        out_specs = [pl.BlockSpec((rows, block), lambda i: (0, i))] * count
        scratch = [pltpu.VMEM((tokens, block), F32)]
    else:
        out_shape = jax.ShapeDtypeStruct((tokens, width), F32)
        out_specs = pl.BlockSpec((tokens, block), lambda i: (0, i))
        scratch = []
    return pl.pallas_call(
        kernel,
        grid=(width // block,),
        out_shape=out_shape,
        in_specs=specs,
        out_specs=out_specs,
        scratch_shapes=scratch,
        compiler_params=params(),
        cost_estimate=cost(4 * tokens * units * width, 4 * units * width),
        name="input_grads",
    )(*operands)


def weight_grads(mine, other, in_all, before, chunk, chunks):
    _, half, units = mine.shape
    tokens, width = in_all.shape
    block = divisor(width, 512)

    def kernel(*refs):
        a, b, x = refs[:3]
        for i, out in enumerate(refs[-2:]):
            grads = jnp.concatenate([a[i], b[i]], axis=0)
            out[...] = lax.dot_general(x[...], grads, TN, preferred_element_type=F32).astype(BF16)

    specs = [pl.BlockSpec((2, half, units), lambda i: (0, 0, 0))] * 2
    specs += [pl.BlockSpec((tokens, block), lambda i: (0, i))]
    operands = [mine, other, in_all]
    aliases = {}
    if before is not None:
        operands += list(before)
        specs += [pl.BlockSpec(memory_space=pl.ANY)] * 2
        aliases = {3: 0, 4: 1}
    shape = jax.ShapeDtypeStruct((width, units * chunks), BF16)
    return pl.pallas_call(
        kernel,
        grid=(width // block,),
        out_shape=(shape, shape),
        in_specs=specs,
        out_specs=[pl.BlockSpec((block, units), lambda i: (i, chunk))] * 2,
        input_output_aliases=aliases,
        compiler_params=params(),
        cost_estimate=cost(4 * tokens * units * width, 4 * units * width),
        name="weight_grads",
    )(*operands)


def after(value, *others):
    return lax.optimization_barrier((value, *others))[0]


def local(nr, nc, inputs, grad_out, gate, up, gate_weight, up_weight, down_weight):
    nx = nr // CORES
    row, col = lax.axis_index("row"), lax.axis_index("col")
    x, core = row // CORES, row % CORES
    own_tokens = gate.shape[0]
    col_tokens = grad_out.shape[0]
    units = down_weight.shape[0]
    chunks = 3 if units % 384 == 0 else 1
    direct = nc == 8 and nr * own_tokens == nc * col_tokens and own_tokens % col_tokens == 0

    def swap_core(value):
        return lax.ppermute(value, "row", [(r, r ^ 1) for r in range(nr)])

    def from_x(value, offset):
        return lax.ppermute(value, "row", [((r + offset * CORES) % nr, r) for r in range(nr)])

    def swap_col(value, mask):
        return lax.ppermute(value, "col", [(c, c ^ mask) for c in range(nc)])

    def place(block):
        block_x, block_core = block // CORES, block % CORES
        return ((block_core ^ core) * nx + (block_x - x + nx) % nx) * own_tokens

    if direct:
        rows = col_tokens
        per = own_tokens // col_tokens
        places = [
            place((col ^ m) // per) + ((col ^ m) % per) * col_tokens for m in range(nc)
        ]
    else:
        rows = own_tokens
        places = [place(r) for r in range(nr)]
    offsets = jnp.stack(places).astype(jnp.int32)

    def gather(value):
        if not direct:
            whole = lax.all_gather(value, "col", axis=0, tiled=True)
            return [whole[r * rows : (r + 1) * rows] for r in range(nr)]
        got = {0: value}
        for m in (1, 2, 4, 6):
            got[m] = swap_col(value, m)
        for m in (2, 4, 6):
            got[m + 1] = swap_col(got[m], 1)
        return [got[m] for m in range(nc)]

    def scatter(blocks):
        if not direct:
            return lax.psum_scatter(
                jnp.concatenate(blocks, axis=0), "col", scatter_dimension=0, tiled=True
            )
        summed = {}
        for m in (6, 4, 2, 0):
            other = swap_col(blocks[m + 1], 1)
            summed[m] = blocks[m].astype(F32) + other.astype(F32)
        total = summed[0]
        for m in (6, 4, 2):
            total = total + swap_col(summed[m].astype(BF16), m).astype(F32)
        return total.astype(BF16)

    gates = [gate] + [from_x(gate, o) for o in range(1, nx)]
    ups = [up] + [from_x(up, o) for o in range(1, nx)]

    out_blocks = gather(grad_out)
    out_all = assemble(out_blocks, offsets)

    sums = []
    for c in range(chunks):
        keep, send = partial_hidden(out_all, down_weight, c, chunks)
        total = (keep.astype(F32) + swap_core(send).astype(F32)).astype(BF16)
        sums.append([total] + [from_x(total, o) for o in range(1, nx)])

    in_all = assemble(gather(after(inputs, out_all)), offsets)

    hidden = activations(gates, ups)
    grad_down = down_grad(hidden, swap_core(hidden), out_all)

    total, weights = None, None
    for c in range(chunks):
        mine = hidden_grads(sums[c], gates, ups, c)
        other = swap_core(mine)
        last = c == chunks - 1
        total = input_grads(
            mine, other, gate_weight, up_weight, total, offsets if last else None, c, rows
        )
        weights = weight_grads(mine, other, in_all, weights, c, chunks)
    grad_inputs = scatter(total)
    return grad_inputs, weights[0], weights[1], grad_down


def solution(mesh):
    return jax.shard_map(
        functools.partial(local, mesh.shape["row"], mesh.shape["col"]),
        mesh=mesh,
        in_specs=(
            P("col", "row"),
            P("col", "row"),
            P("row", "col"),
            P("row", "col"),
            P("row", "col"),
            P("row", "col"),
            P("col", "row"),
        ),
        out_specs=(P("col", "row"), P("row", "col"), P("row", "col"), P("col", "row")),
        check_vma=False,
    )
```

```python
import functools
import math

import jax
import jax.numpy as jnp
from jax import lax
from jax.experimental import pallas as pl
from jax.experimental.pallas import tpu as pltpu
from jax.sharding import PartitionSpec as P

F32 = jnp.float32
BF16 = jnp.bfloat16
CORES = 2
VMEM = 10 * 2**20
ANYWHERE = pl.BlockSpec(memory_space=pl.ANY)
REMAIN = pl.BlockSpec(memory_space=pltpu.HBM)
RESIDENT = pl.BlockSpec(memory_space=pltpu.VMEM)
SCALARS = pl.BlockSpec(memory_space=pltpu.SMEM)
WHOLE = pl.BlockSpec(memory_space=pltpu.VMEM)
NT = (((1,), (1,)), ((), ()))
TN = (((0,), (0,)), ((), ()))


def divisor(size, target, step=128):
    best = size
    for cand in range(step, target + 1, step):
        if size % cand == 0:
            best = cand
    return best


def call(kernel, operands, in_specs, out_shape, out_specs, deps=(), scratch=(), aliases=None, **kwargs):
    given = len(operands)
    total = given + len(deps)
    kept = {id(REMAIN): pltpu.HBM, id(RESIDENT): pltpu.VMEM}
    operands = [
        pltpu.with_memory_space_constraint(operand, kept[id(spec)]) if id(spec) in kept else operand
        for operand, spec in zip(operands, in_specs)
    ]

    held = sum(math.prod(s.shape) * s.dtype.itemsize for s in scratch if s.memory_space is pltpu.VMEM)

    def body(*refs):
        kernel(*refs[:given], *refs[total:])

    return pl.pallas_call(
        body,
        out_shape=out_shape,
        in_specs=list(in_specs) + [ANYWHERE] * len(deps),
        out_specs=out_specs,
        scratch_shapes=list(scratch),
        input_output_aliases=aliases or {},
        compiler_params=pltpu.CompilerParams(vmem_limit_bytes=VMEM + held),
        **kwargs,
    )(*operands, *deps)


def lay(blocks, offs, out, rows, first=0):
    i = first
    for block in blocks:
        for lo in range(0, block.shape[0], rows):
            out[pl.ds(pl.multiple_of(offs[i], rows), rows), :] = block[lo : lo + rows, :]
            i += 1


def assemble(blocks, offsets, deps=()):
    count, width = len(blocks), blocks[0].shape[1]
    tokens = sum(block.shape[0] for block in blocks)
    rows = tokens // offsets.shape[0]

    def kernel(offs, *refs):
        lay(refs[:count], offs, refs[count], rows)

    return call(
        kernel,
        [offsets, *blocks],
        [SCALARS] + [WHOLE] * count,
        jax.ShapeDtypeStruct((tokens, width), BF16),
        WHOLE,
        deps,
        name="assemble",
    )


def copies_of(weight, lo, units, piece, ready, sems):
    copies = []
    for i in range(units // piece):
        at = pl.ds(i * piece, piece)
        copies.append(
            pltpu.make_async_copy(weight.at[pl.ds(lo + i * piece, piece)], ready.at[at], sems.at[i])
        )
        copies[-1].start()
    return copies


def dots_of(a, copies, piece, ready, keep, send):
    half = keep.shape[0]
    for i, copy in enumerate(copies):
        copy.wait()
        at = slice(i * piece, (i + 1) * piece)
        part = lax.dot_general(a[...], ready[at, :], NT, preferred_element_type=F32).astype(BF16)
        keep[:, at] = part[:half]
        send[:, at] = part[half:]


def first_partial(blocks, offsets, down, span, deps=()):
    count, width = len(blocks), blocks[0].shape[1]
    tokens = sum(block.shape[0] for block in blocks)
    run = tokens // offsets.shape[0]
    lo, units = span
    piece = divisor(units, 640)
    pieces = units // piece

    def kernel(offs, *refs):
        own, others, weight = refs[0], refs[1:count], refs[count]
        keep, send, a, ready, sems = refs[count + 1 :]
        moves = []
        if count > 1:
            at = pl.ds(pl.multiple_of(offs[0], run), run)
            moves.append(pltpu.make_async_copy(own, a.at[at], sems.at[pieces]))
            moves[0].start()
        copies = copies_of(weight, lo, units, piece, ready, sems)
        lay(others if count > 1 else [own], offs, a, run, 1 if count > 1 else 0)
        for move in moves:
            move.wait()
        dots_of(a, copies, piece, ready, keep, send)

    part = jax.ShapeDtypeStruct((tokens // CORES, units), BF16)
    return call(
        kernel,
        [offsets, *blocks, down],
        [SCALARS, REMAIN if count > 1 else WHOLE] + [WHOLE] * (count - 1) + [REMAIN],
        (part, part, jax.ShapeDtypeStruct((tokens, width), BF16)),
        [WHOLE] * 3,
        deps,
        scratch=[pltpu.VMEM((units, width), BF16), pltpu.SemaphoreType.DMA((pieces + 1,))],
        name="first_partial",
    )


def activations(gates, ups, deps=()):
    count = len(gates)
    rows, width = gates[0].shape

    def kernel(*refs):
        out = refs[2 * count]
        for i in range(count):
            gate = refs[i][...].astype(F32)
            up = refs[count + i][...].astype(F32)
            out[i * rows : (i + 1) * rows, :] = (gate * jax.nn.sigmoid(gate) * up).astype(BF16)

    return call(
        kernel,
        [*gates, *ups],
        [WHOLE] * (2 * count),
        jax.ShapeDtypeStruct((rows * count, width), BF16),
        WHOLE,
        deps,
        name="activations",
    )


def hidden_grads(sums, gates, ups, span, passed=(), deps=()):
    count = len(gates)
    rows = gates[0].shape[0]
    lo, units = span
    cols = slice(lo, lo + units)

    def kernel(*refs):
        out = refs[3 * count + len(passed)]
        for i in range(count):
            grad = 0.0
            for o in range(count):
                j = (i - o) % count
                grad = grad + refs[o][j * rows : (j + 1) * rows, :].astype(F32)
            gate = refs[count + i][:, cols].astype(F32)
            up = refs[2 * count + i][:, cols].astype(F32)
            sig = jax.nn.sigmoid(gate)
            at = slice(i * rows, (i + 1) * rows)
            out[0, at, :] = (grad * up * sig * (1.0 + gate * (1.0 - sig))).astype(BF16)
            out[1, at, :] = (grad * gate * sig).astype(BF16)

    shapes = [jax.ShapeDtypeStruct((2, rows * count, units), BF16)]
    shapes += [jax.ShapeDtypeStruct(p.shape, p.dtype) for p in passed]
    return call(
        kernel,
        [*sums, *gates, *ups, *passed],
        [WHOLE] * (3 * count) + [ANYWHERE] * len(passed),
        shapes,
        [WHOLE] + [ANYWHERE] * len(passed),
        deps,
        aliases={3 * count + i: 1 + i for i in range(len(passed))},
        name="hidden_grads",
    )


def both(mine, other, *at):
    return jnp.concatenate([mine[at], other[at]], axis=0)


def down_grad(hidden, hidden_other, out_all, down=None, span=(0, 0), deps=()):
    half, units = hidden.shape
    tokens, width = out_all.shape
    piece = divisor(units, 256)
    count = units // piece
    slots = min(8, count)
    lo, taken = span
    operands, specs = [hidden, hidden_other, out_all], [WHOLE] * 3
    shapes = [jax.ShapeDtypeStruct((units, width), BF16), jax.ShapeDtypeStruct((8, 128), F32)]
    scratch = [pltpu.VMEM((slots, piece, width), BF16), pltpu.SemaphoreType.DMA((slots,))]
    if taken:
        operands.append(down)
        specs.append(REMAIN)
        shapes += [jax.ShapeDtypeStruct((half, taken), BF16)] * 2
        run = divisor(taken, 640)
        scratch += [pltpu.VMEM((taken, width), BF16), pltpu.SemaphoreType.DMA((taken // run,))]

    def kernel(*refs):
        a, b, g = refs[:3]
        given = len(operands)
        out, token = refs[given : given + 2]
        ready, sems = refs[given + len(shapes) : given + len(shapes) + 2]
        token[...] = jnp.zeros(token.shape, F32)
        if taken:
            copies = copies_of(refs[3], lo, taken, run, refs[-2], refs[-1])
        stores = []
        for i in range(count):
            at, slot = slice(i * piece, (i + 1) * piece), i % slots
            if i >= slots:
                stores[i - slots].wait()
            ready[slot] = lax.dot_general(
                both(a, b, slice(None), at), g[...], TN, preferred_element_type=F32
            ).astype(BF16)
            store = pltpu.make_async_copy(ready.at[slot], out.at[at], sems.at[slot])
            store.start()
            stores.append(store)
        if taken:
            dots_of(g, copies, run, refs[-2], refs[given + 2], refs[given + 3])
        for store in stores[count - slots :]:
            store.wait()

    return call(
        kernel,
        operands,
        specs,
        shapes,
        [REMAIN] + [WHOLE] * (len(shapes) - 1),
        deps,
        scratch=scratch,
        name="down_grad",
    )


def input_grads(mine, other, gate_weight, up_weight, before, offsets, span, rows, groups, deps=()):
    _, half, units = mine.shape
    tokens = 2 * half
    width = gate_weight.shape[0]
    piece = divisor(width, 512)
    pieces = width // piece
    slots = min(4, pieces)
    cols = slice(span[0], span[0] + units)
    operands = [offsets, mine, other, gate_weight, up_weight] + ([] if before is None else [before])
    specs = [SCALARS, WHOLE, WHOLE, REMAIN, REMAIN] + ([] if before is None else [WHOLE])
    if groups is None:
        shapes = [jax.ShapeDtypeStruct((tokens, width), F32)]
    else:
        shapes = [jax.ShapeDtypeStruct((rows * len(group), width), BF16) for group in groups]

    def kernel(*refs):
        offs, a, b, gw, uw = refs[:5]
        outs = refs[len(operands) : len(operands) + len(shapes)]
        sums, ready, sems = refs[-3:]
        copies = []
        for j in range(pieces):
            at = slice(j * piece, (j + 1) * piece)
            for i, w in enumerate((gw, uw)):
                copies.append(
                    pltpu.make_async_copy(
                        w.at[at, cols], ready.at[i, j % slots], sems.at[i, j % slots]
                    )
                )
        for copy in copies[: 2 * slots]:
            copy.start()
        for j in range(pieces):
            at = slice(j * piece, (j + 1) * piece)
            total = 0.0 if before is None else refs[5][:, at]
            for i in range(2):
                copies[2 * j + i].wait()
            for i in range(2):
                total = total + lax.dot_general(
                    both(a, b, i), ready[i, j % slots], NT, preferred_element_type=F32
                )
            sums[:, at] = total
            for copy in copies[2 * (j + slots) : 2 * (j + slots + 1)]:
                copy.start()
        if groups is None:
            outs[0][...] = sums[...]
        for out, group in zip(outs, groups or ()):
            for i, m in enumerate(group):
                at = pl.ds(pl.multiple_of(offs[m], rows), rows)
                out[i * rows : (i + 1) * rows, :] = sums[at, :].astype(BF16)

    return call(
        kernel,
        operands,
        specs,
        shapes,
        [WHOLE] * len(shapes),
        deps,
        scratch=[
            pltpu.VMEM((tokens, width), F32),
            pltpu.VMEM((2, slots, piece, units), BF16),
            pltpu.SemaphoreType.DMA((2, slots)),
        ],
        name="input_grads",
    )


def fold(own, other, deps=()):
    rows, width = own.shape[0] // 2, own.shape[1]

    def kernel(a, b, *outs):
        for i, out in enumerate(outs[:2]):
            at = slice(i * rows, (i + 1) * rows)
            total = a[at, :].astype(F32) + b[at, :].astype(F32)
            out[...] = total.astype(BF16)
        outs[2][...] = total

    shape = (rows, width)
    return call(
        kernel,
        [own, other],
        [WHOLE] * 2,
        (
            jax.ShapeDtypeStruct(shape, BF16),
            jax.ShapeDtypeStruct(shape, BF16),
            jax.ShapeDtypeStruct(shape, F32),
        ),
        [WHOLE] * 3,
        deps,
        name="fold",
    )


def weight_grads(mine, other, in_all, before, start, span, whole, deps=()):
    skip, units = span[0] - start, span[1]
    tokens, width = in_all.shape
    piece = divisor(width, 256)
    count = width // piece
    slots = min(8, count)
    cols = slice(span[0], span[0] + units)

    def kernel(*refs):
        a, b, x = refs[:3]
        outs, token, ready, sems = refs[-5:-3], refs[-3], refs[-2], refs[-1]
        token[...] = jnp.zeros(token.shape, F32)
        taken = slice(skip, skip + units)
        copies = []
        for j in range(count):
            at, slot = slice(j * piece, (j + 1) * piece), j % slots
            for i in range(2):
                if j >= slots:
                    copies[2 * (j - slots) + i].wait()
                ready[i, slot] = lax.dot_general(
                    x[:, at], both(a, b, i, slice(None), taken), TN, preferred_element_type=F32
                ).astype(BF16)
                copy = pltpu.make_async_copy(
                    ready.at[i, slot], outs[i].at[at, cols], sems.at[i, slot]
                )
                copy.start()
                copies.append(copy)
        for copy in copies[2 * (count - slots) :]:
            copy.wait()

    shape = jax.ShapeDtypeStruct((width, whole), BF16)
    return call(
        kernel,
        [mine, other, in_all, *(before or ())],
        [WHOLE] * 3 + [REMAIN] * (2 if before else 0),
        (shape, shape, jax.ShapeDtypeStruct((8, 128), F32)),
        [REMAIN, REMAIN, WHOLE],
        deps,
        scratch=[
            pltpu.VMEM((2, slots, piece, units), BF16),
            pltpu.SemaphoreType.DMA((2, slots)),
        ],
        aliases={3: 0, 4: 1} if before else None,
        name="weight_grads",
    )


def local(nr, nc, inputs, grad_out, gate, up, gate_weight, up_weight, down_weight):
    nx = nr // CORES
    row, col = lax.axis_index("row"), lax.axis_index("col")
    x, core = row // CORES, row % CORES
    own_tokens = gate.shape[0]
    col_tokens = grad_out.shape[0]
    units = down_weight.shape[0]
    first = units // 3 * 2 if units % 384 == 0 else units
    spans = [(0, first)] + ([(first, units - first)] if first < units else [])
    direct = nc == 8 and nr * own_tokens == nc * col_tokens and own_tokens % col_tokens == 0

    def swap_core(value):
        return lax.ppermute(value, "row", [(r, r ^ 1) for r in range(nr)])

    def from_x(value, offset):
        return lax.ppermute(value, "row", [((r + offset * CORES) % nr, r) for r in range(nr)])

    def swap_col(value, mask):
        return lax.ppermute(value, "col", [(c, c ^ mask) for c in range(nc)])

    def place(block):
        block_x, block_core = block // CORES, block % CORES
        return ((block_core ^ core) * nx + (block_x - x + nx) % nx) * own_tokens

    in_order = jnp.stack([place(r) for r in range(nr)]).astype(jnp.int32)
    if direct:
        rows, per = col_tokens, own_tokens // col_tokens
        places = [place((col ^ m) // per) + ((col ^ m) % per) * rows for m in range(nc)]
        offsets = jnp.stack(places).astype(jnp.int32)
    else:
        rows, offsets = own_tokens, in_order

    def gather(value):
        if not direct:
            return [lax.all_gather(value, "col", axis=0, tiled=True)]
        got = {0: value}
        got[1] = swap_col(value, 1)
        got[4] = swap_col(value, 4)
        got[2] = swap_col(value, 2)
        got[3] = swap_col(got[1], 2)
        got[6] = swap_col(got[4], 2)
        got[5] = swap_col(got[4], 1)
        got[7] = swap_col(got[6], 1)
        return [got[m] for m in range(nc)]

    gates = [gate] + [from_x(gate, o) for o in range(1, nx)]
    ups = [up] + [from_x(up, o) for o in range(1, nx)]

    def exchanged(keep, send):
        total = (keep.astype(F32) + swap_core(send).astype(F32)).astype(BF16)
        return [total] + [from_x(total, o) for o in range(1, nx)]

    out_blocks = gather(grad_out)
    hidden = activations(gates, ups, deps=out_blocks[-2:-1])
    keep, send, out_all = first_partial(
        out_blocks, offsets, down_weight, spans[0], deps=[hidden]
    )
    hidden_other = swap_core(hidden)
    sums = [exchanged(keep, send)]
    if direct:
        own = jnp.concatenate([inputs, swap_col(inputs, 1)], axis=0)
        in_blocks = [own, swap_col(own, 2), swap_col(own, 4)]
    else:
        own = sums[0][0]
        in_blocks = [lax.all_gather(inputs, "col", axis=0, tiled=True)]
    span = spans[1] if len(spans) > 1 else (0, 0)
    grad_down, token, *parts = down_grad(
        hidden, hidden_other, out_all, down_weight, span, deps=[sums[0][0], own]
    )

    mine, *parts = hidden_grads(sums[0], gates, ups, spans[0], parts, [token, *in_blocks])
    grads = [(mine, swap_core(mine))]
    groups = [(7, 5), (3, 1), (6, 4), (2, 0)] if direct else [range(nr)]
    if direct:
        in_blocks.append(swap_col(in_blocks[2], 2))
    total = None
    if len(spans) > 1:
        sums.append(exchanged(*parts))
        (total,) = input_grads(
            *grads[0], gate_weight, up_weight, None, offsets, spans[0], rows, None, sums[1][:1]
        )
        (mine,) = hidden_grads(sums[1], gates, ups, spans[1], deps=[total, *in_blocks])
        grads.append((mine, swap_core(mine)))
    blocks = input_grads(
        *grads[-1], gate_weight, up_weight, total, offsets, spans[-1], rows, groups
    )
    in_all = assemble(in_blocks, offsets if direct else in_order, deps=blocks[:1])

    def weight_part(before, i, span, deps):
        *weights, token = weight_grads(
            *grads[i], in_all, before, spans[i][0], span, units, deps
        )
        return weights, token

    cut = divisor(first, first // 2)
    weights, token = weight_part(None, 0, (0, cut), [])
    if direct:
        far, near = swap_col(blocks[0], 1), swap_col(blocks[1], 1)
        sent6, sent4, _ = fold(blocks[2], far, deps=[token])
        part6, part4 = swap_col(sent6, 6), swap_col(sent4, 4)
        ready = sent4
    else:
        ready = blocks[0]
    if cut < first:
        weights, token = weight_part(weights, 0, (cut, first - cut), [ready])
    if direct:
        sent2, _, result = fold(blocks[3], near, deps=[token, part6])
        part2 = swap_col(sent2, 2)
        ready = sent2
    if len(spans) > 1:
        weights, token = weight_part(weights, 1, spans[1], [ready])
    if direct:
        for part in (part6, part4, part2):
            result = result + part.astype(F32)
        grad_inputs = result.astype(BF16)
    else:
        grad_inputs = lax.psum_scatter(blocks[0], "col", scatter_dimension=0, tiled=True)
    return grad_inputs, *weights, grad_down


def solution(mesh):
    return jax.shard_map(
        functools.partial(local, mesh.shape["row"], mesh.shape["col"]),
        mesh=mesh,
        in_specs=(
            P("col", "row"),
            P("col", "row"),
            P("row", "col"),
            P("row", "col"),
            P("row", "col"),
            P("row", "col"),
            P("col", "row"),
        ),
        out_specs=(P("col", "row"), P("row", "col"), P("row", "col"), P("col", "row")),
        check_vma=False,
    )
```

```python
import functools
import math

import jax
import jax.numpy as jnp
from jax import lax
from jax.experimental import pallas as pl
from jax.experimental.pallas import tpu as pltpu
from jax.sharding import PartitionSpec as P

F32 = jnp.float32
BF16 = jnp.bfloat16
CORES = 2
VMEM = 10 * 2**20
ANYWHERE = pl.BlockSpec(memory_space=pl.ANY)
REMAIN = pl.BlockSpec(memory_space=pltpu.HBM)
RESIDENT = pl.BlockSpec(memory_space=pltpu.VMEM)
SCALARS = pl.BlockSpec(memory_space=pltpu.SMEM)
WHOLE = pl.BlockSpec(memory_space=pltpu.VMEM)
NT = (((1,), (1,)), ((), ()))
TN = (((0,), (0,)), ((), ()))


def divisor(size, target, step=128):
    best = size
    for cand in range(step, target + 1, step):
        if size % cand == 0:
            best = cand
    return best


def call(kernel, operands, in_specs, out_shape, out_specs, deps=(), scratch=(), aliases=None, **kwargs):
    given = len(operands)
    total = given + len(deps)
    kept = {id(REMAIN): pltpu.HBM, id(RESIDENT): pltpu.VMEM}
    operands = [
        pltpu.with_memory_space_constraint(operand, kept[id(spec)]) if id(spec) in kept else operand
        for operand, spec in zip(operands, in_specs)
    ]

    held = sum(math.prod(s.shape) * s.dtype.itemsize for s in scratch if s.memory_space is pltpu.VMEM)

    def body(*refs):
        kernel(*refs[:given], *refs[total:])

    return pl.pallas_call(
        body,
        out_shape=out_shape,
        in_specs=list(in_specs) + [ANYWHERE] * len(deps),
        out_specs=out_specs,
        scratch_shapes=list(scratch),
        input_output_aliases=aliases or {},
        compiler_params=pltpu.CompilerParams(vmem_limit_bytes=VMEM + held),
        **kwargs,
    )(*operands, *deps)


def lay(blocks, offs, out, rows, first=0):
    i = first
    for block in blocks:
        for lo in range(0, block.shape[0], rows):
            out[pl.ds(pl.multiple_of(offs[i], rows), rows), :] = block[lo : lo + rows, :]
            i += 1


def assemble(blocks, offsets, deps=()):
    count, width = len(blocks), blocks[0].shape[1]
    tokens = sum(block.shape[0] for block in blocks)
    rows = tokens // offsets.shape[0]

    def kernel(offs, *refs):
        lay(refs[:count], offs, refs[count], rows)

    return call(
        kernel,
        [offsets, *blocks],
        [SCALARS] + [WHOLE] * count,
        jax.ShapeDtypeStruct((tokens, width), BF16),
        WHOLE,
        deps,
        name="assemble",
    )


def fetch(weight, span, others, deps=()):
    lo, units = span
    arrays = [weight, *others]
    shapes = [(units, weight.shape[1]), *(o.shape for o in others)]

    def kernel(*refs):
        given, outs, sems = refs[: len(arrays)], refs[len(arrays) : -1], refs[-1]
        copies = []
        for i, (source, out) in enumerate(zip(given, outs)):
            if i == 0:
                source = source.at[pl.ds(lo, units)]
            copies.append(pltpu.make_async_copy(source, out, sems.at[i]))
            copies[-1].start()
        for copy in copies:
            copy.wait()

    return call(
        kernel,
        arrays,
        [REMAIN] * len(arrays),
        [pltpu.VMEM(shape, BF16) for shape in shapes],
        [WHOLE] * len(arrays),
        deps,
        scratch=[pltpu.SemaphoreType.DMA((len(arrays),))],
        name="fetch",
    )


def run_copy(weight, lo, i, piece, ready, sems):
    at = pl.ds(pl.multiple_of(i * piece, piece), piece)
    return pltpu.make_async_copy(
        weight.at[pl.ds(pl.multiple_of(lo + i * piece, piece), piece)], ready.at[at], sems.at[i]
    )


def start_copies(weight, lo, count, piece, ready, sems):
    for i in range(count):
        run_copy(weight, lo, i, piece, ready, sems).start()


def dots_of(a, weight, lo, count, piece, ready, sems, keep, send):
    half = keep.shape[0]

    def step(i, carry):
        run_copy(weight, lo, i, piece, ready, sems).wait()
        at = pl.ds(pl.multiple_of(i * piece, piece), piece)
        part = lax.dot_general(a[...], ready[at, :], NT, preferred_element_type=F32).astype(BF16)
        keep[:, at] = part[:half]
        send[:, at] = part[half:]
        return carry

    lax.fori_loop(0, count, step, 0)


def first_partial(blocks, offsets, rows, deps=()):
    count, width = len(blocks), blocks[0].shape[1]
    tokens = sum(block.shape[0] for block in blocks)
    run = tokens // offsets.shape[0]
    half, units = tokens // CORES, rows.shape[0]
    piece = divisor(units, 640, 256)

    def kernel(offs, *refs):
        weight, keep, send, a = refs[count:]
        lay(refs[:count], offs, a, run)
        for lo in range(0, units, piece):
            at = slice(lo, lo + piece)
            part = lax.dot_general(a[...], weight[at, :], NT, preferred_element_type=F32)
            part = part.astype(BF16)
            keep[:, at] = part[:half]
            send[:, at] = part[half:]

    part = jax.ShapeDtypeStruct((half, units), BF16)
    return call(
        kernel,
        [offsets, *blocks, rows],
        [SCALARS] + [WHOLE] * count + [RESIDENT],
        (part, part, jax.ShapeDtypeStruct((tokens, width), BF16)),
        [WHOLE] * 3,
        deps,
        name="first_partial",
    )


def activations(gates, ups, deps=()):
    count = len(gates)
    rows, width = gates[0].shape

    def kernel(*refs):
        out = refs[2 * count]
        for i in range(count):
            gate = refs[i][...].astype(F32)
            up = refs[count + i][...].astype(F32)
            out[i * rows : (i + 1) * rows, :] = (gate * jax.nn.sigmoid(gate) * up).astype(BF16)

    return call(
        kernel,
        [*gates, *ups],
        [WHOLE] * (2 * count),
        jax.ShapeDtypeStruct((rows * count, width), BF16),
        WHOLE,
        deps,
        name="activations",
    )


def hidden_grads(sums, gates, ups, span, passed=(), deps=()):
    count = len(gates)
    rows = gates[0].shape[0]
    lo, units = span
    cols = slice(lo, lo + units)

    def kernel(*refs):
        out = refs[3 * count + len(passed)]
        for i in range(count):
            grad = 0.0
            for o in range(count):
                j = (i - o) % count
                grad = grad + refs[o][j * rows : (j + 1) * rows, :].astype(F32)
            gate = refs[count + i][:, cols].astype(F32)
            up = refs[2 * count + i][:, cols].astype(F32)
            sig = jax.nn.sigmoid(gate)
            at = slice(i * rows, (i + 1) * rows)
            out[0, at, :] = (grad * up * sig * (1.0 + gate * (1.0 - sig))).astype(BF16)
            out[1, at, :] = (grad * gate * sig).astype(BF16)

    shapes = [jax.ShapeDtypeStruct((2, rows * count, units), BF16)]
    shapes += [jax.ShapeDtypeStruct(p.shape, p.dtype) for p in passed]
    return call(
        kernel,
        [*sums, *gates, *ups, *passed],
        [WHOLE] * (3 * count) + [ANYWHERE] * len(passed),
        shapes,
        [WHOLE] + [ANYWHERE] * len(passed),
        deps,
        aliases={3 * count + i: 1 + i for i in range(len(passed))},
        name="hidden_grads",
    )


def both(mine, other, *at):
    return jnp.concatenate([mine[at], other[at]], axis=0)


def down_grad(hidden, hidden_other, out_all, down=None, span=(0, 0), deps=()):
    half, units = hidden.shape
    tokens, width = out_all.shape
    piece = divisor(units, 640)
    count = units // piece
    slots = min(3, count)
    lo, taken = span
    operands, specs = [hidden, hidden_other, out_all], [WHOLE] * 3
    shapes = [jax.ShapeDtypeStruct((units, width), BF16), jax.ShapeDtypeStruct((8, 128), F32)]
    scratch = [pltpu.VMEM((slots, piece, width), BF16), pltpu.SemaphoreType.DMA((slots,))]
    if taken:
        operands.append(down)
        specs.append(REMAIN)
        shapes += [jax.ShapeDtypeStruct((half, taken), BF16)] * 2
        run = divisor(taken, 1280)
        scratch += [pltpu.VMEM((taken, width), BF16), pltpu.SemaphoreType.DMA((taken // run,))]

    def kernel(*refs):
        a, b, g = refs[:3]
        given = len(operands)
        out, token = refs[given : given + 2]
        ready, sems = refs[given + len(shapes) : given + len(shapes) + 2]
        token[...] = jnp.zeros(token.shape, F32)
        if taken:
            start_copies(refs[3], lo, taken // run, run, refs[-2], refs[-1])

        def store(i):
            slot = lax.rem(i, slots)
            at = pl.ds(pl.multiple_of(i * piece, piece), piece)
            return pltpu.make_async_copy(ready.at[slot], out.at[at], sems.at[slot])

        def step(i, carry):
            @pl.when(i >= slots)
            def _():
                store(i - slots).wait()

            at = pl.ds(pl.multiple_of(i * piece, piece), piece)
            ready[lax.rem(i, slots)] = lax.dot_general(
                both(a, b, slice(None), at), g[...], TN, preferred_element_type=F32
            ).astype(BF16)
            store(i).start()
            return carry

        lax.fori_loop(0, count, step, 0)
        if taken:
            dots_of(
                g, refs[3], lo, taken // run, run, refs[-2], refs[-1], refs[given + 2], refs[given + 3]
            )
        for i in range(count - slots, count):
            store(i).wait()

    return call(
        kernel,
        operands,
        specs,
        shapes,
        [REMAIN] + [WHOLE] * (len(shapes) - 1),
        deps,
        scratch=scratch,
        name="down_grad",
    )


def input_grads(mine, other, gate_weight, up_weight, before, offsets, span, rows, groups, deps=()):
    _, half, units = mine.shape
    tokens = 2 * half
    width = gate_weight.shape[0]
    piece = divisor(width, 512)
    pieces = width // piece
    slots = min(4, pieces)
    cols = slice(span[0], span[0] + units)
    operands = [offsets, mine, other, gate_weight, up_weight] + ([] if before is None else [before])
    specs = [SCALARS, WHOLE, WHOLE, REMAIN, REMAIN] + ([] if before is None else [WHOLE])
    if groups is None:
        shapes = [jax.ShapeDtypeStruct((tokens, width), F32)]
    else:
        shapes = [jax.ShapeDtypeStruct((rows * len(group), width), BF16) for group in groups]

    def kernel(*refs):
        offs, a, b, gw, uw = refs[:5]
        outs = refs[len(operands) : len(operands) + len(shapes)]
        sums, ready, sems = refs[-3:]
        copies = []
        for j in range(pieces):
            at = slice(j * piece, (j + 1) * piece)
            for i, w in enumerate((gw, uw)):
                copies.append(
                    pltpu.make_async_copy(
                        w.at[at, cols], ready.at[i, j % slots], sems.at[i, j % slots]
                    )
                )
        for copy in copies[: 2 * slots]:
            copy.start()
        for j in range(pieces):
            at = slice(j * piece, (j + 1) * piece)
            total = 0.0 if before is None else refs[5][:, at]
            for i in range(2):
                copies[2 * j + i].wait()
            for i in range(2):
                total = total + lax.dot_general(
                    both(a, b, i), ready[i, j % slots], NT, preferred_element_type=F32
                )
            sums[:, at] = total
            for copy in copies[2 * (j + slots) : 2 * (j + slots + 1)]:
                copy.start()
        if groups is None:
            outs[0][...] = sums[...]
        for out, group in zip(outs, groups or ()):
            for i, m in enumerate(group):
                at = pl.ds(pl.multiple_of(offs[m], rows), rows)
                out[i * rows : (i + 1) * rows, :] = sums[at, :].astype(BF16)

    return call(
        kernel,
        operands,
        specs,
        shapes,
        [WHOLE] * len(shapes),
        deps,
        scratch=[
            pltpu.VMEM((tokens, width), F32),
            pltpu.VMEM((2, slots, piece, units), BF16),
            pltpu.SemaphoreType.DMA((2, slots)),
        ],
        name="input_grads",
    )


def fold(terms, wide, deps=()):
    arrays, refs_of = [], []
    for term in terms:
        refs_of.append([])
        for array, row in term:
            known = [i for i, a in enumerate(arrays) if a is array]
            if not known:
                arrays.append(array)
            refs_of[-1].append((known[0] if known else len(arrays) - 1, row))
    rows, width = min(a.shape[0] for a in arrays), arrays[0].shape[1]
    kinds = [F32 if w else BF16 for w in wide]

    def kernel(*refs):
        for out, pairs in zip(refs[len(arrays) :], refs_of):
            total = 0.0
            for i, row in pairs:
                total = total + refs[i][row * rows : (row + 1) * rows, :].astype(F32)
            out[...] = total.astype(out.dtype)

    return call(
        kernel,
        arrays,
        [WHOLE] * len(arrays),
        [jax.ShapeDtypeStruct((rows, width), kind) for kind in kinds],
        [WHOLE] * len(terms),
        deps,
        name="fold",
    )


def weight_grads(mine, other, in_all, before, start, span, whole, deps=()):
    skip, units = span[0] - start, span[1]
    tokens, width = in_all.shape
    piece = divisor(width, 256)
    count = width // piece
    slots = min(8, count)
    cols = slice(span[0], span[0] + units)

    def kernel(*refs):
        a, b, x = refs[:3]
        outs, token, ready, sems = refs[-5:-3], refs[-3], refs[-2], refs[-1]
        token[...] = jnp.zeros(token.shape, F32)
        taken = slice(skip, skip + units)
        copies = []
        for j in range(count):
            at, slot = slice(j * piece, (j + 1) * piece), j % slots
            for i in range(2):
                if j >= slots:
                    copies[2 * (j - slots) + i].wait()
                ready[i, slot] = lax.dot_general(
                    x[:, at], both(a, b, i, slice(None), taken), TN, preferred_element_type=F32
                ).astype(BF16)
                copy = pltpu.make_async_copy(
                    ready.at[i, slot], outs[i].at[at, cols], sems.at[i, slot]
                )
                copy.start()
                copies.append(copy)
        for copy in copies[2 * (count - slots) :]:
            copy.wait()

    shape = jax.ShapeDtypeStruct((width, whole), BF16)
    return call(
        kernel,
        [mine, other, in_all, *(before or ())],
        [WHOLE] * 3 + [REMAIN] * (2 if before else 0),
        (shape, shape, jax.ShapeDtypeStruct((8, 128), F32)),
        [REMAIN, REMAIN, WHOLE],
        deps,
        scratch=[
            pltpu.VMEM((2, slots, piece, units), BF16),
            pltpu.SemaphoreType.DMA((2, slots)),
        ],
        aliases={3: 0, 4: 1} if before else None,
        name="weight_grads",
    )


def local(nr, nc, inputs, grad_out, gate, up, gate_weight, up_weight, down_weight):
    nx = nr // CORES
    row, col = lax.axis_index("row"), lax.axis_index("col")
    x, core = row // CORES, row % CORES
    own_tokens = gate.shape[0]
    col_tokens = grad_out.shape[0]
    units = down_weight.shape[0]
    first = units // 5 * 3 if units % 640 == 0 else units
    spans = [(0, first)] + ([(first, units - first)] if first < units else [])
    direct = nc == 8 and nr * own_tokens == nc * col_tokens and own_tokens % col_tokens == 0

    def swap_core(value):
        return lax.ppermute(value, "row", [(r, r ^ 1) for r in range(nr)])

    def from_x(value, offset):
        return lax.ppermute(value, "row", [((r + offset * CORES) % nr, r) for r in range(nr)])

    def swap_col(value, mask):
        return lax.ppermute(value, "col", [(c, c ^ mask) for c in range(nc)])

    def place(block):
        block_x, block_core = block // CORES, block % CORES
        return ((block_core ^ core) * nx + (block_x - x + nx) % nx) * own_tokens

    in_order = jnp.stack([place(r) for r in range(nr)]).astype(jnp.int32)
    if direct:
        rows, per = col_tokens, own_tokens // col_tokens
        places = [place((col ^ m) // per) + ((col ^ m) % per) * rows for m in range(nc)]
        offsets = jnp.stack(places).astype(jnp.int32)
    else:
        rows, offsets = own_tokens, in_order

    def gather(value):
        if not direct:
            return [lax.all_gather(value, "col", axis=0, tiled=True)]
        got = {0: value}
        got[1] = swap_col(value, 1)
        got[4] = swap_col(value, 4)
        got[2] = swap_col(value, 2)
        got[3] = swap_col(got[1], 2)
        got[6] = swap_col(got[4], 2)
        got[5] = swap_col(got[4], 1)
        got[7] = swap_col(got[6], 1)
        return [got[m] for m in range(nc)]

    gates = [gate] + [from_x(gate, o) for o in range(1, nx)]
    ups = [up] + [from_x(up, o) for o in range(1, nx)]

    def exchanged(keep, send):
        total = (keep.astype(F32) + swap_core(send).astype(F32)).astype(BF16)
        return [total] + [from_x(total, o) for o in range(1, nx)]

    blocks = gather(grad_out)
    late = blocks[6:7]
    if direct:
        rows_here, blocks[0], gates[0], ups[0] = fetch(
            down_weight, spans[0], [grad_out, gate, up], deps=late
        )
    else:
        rows_here, gates[0], ups[0] = fetch(down_weight, spans[0], [gate, up])
    beside = [swap_col(inputs, 1)] if direct else []
    keep, send, out_all = first_partial(
        blocks, offsets, rows_here, deps=[*gates[1:], *ups[1:], *beside]
    )
    hidden = activations(gates, ups, deps=[keep])
    hidden_other = swap_core(hidden)
    sums = [exchanged(keep, send)]
    if direct:
        own = jnp.concatenate([inputs, *beside], axis=0)
        in_blocks = [own, swap_col(own, 2), swap_col(own, 4)]
    else:
        own = sums[0][0]
        in_blocks = [lax.all_gather(inputs, "col", axis=0, tiled=True)]
    span = spans[1] if len(spans) > 1 else (0, 0)
    grad_down, token, *parts = down_grad(
        hidden, hidden_other, out_all, down_weight, span, deps=[sums[0][0], own]
    )

    mine, *parts = hidden_grads(sums[0], gates, ups, spans[0], parts, [token, *in_blocks])
    grads = [(mine, swap_core(mine))]
    groups = [(7, 5), (3,), (6, 4, 1), (2,), (0,)] if direct else [range(nr)]
    if direct:
        in_blocks.append(swap_col(in_blocks[2], 2))
    total = None
    if len(spans) > 1:
        sums.append(exchanged(*parts))
        (total,) = input_grads(
            *grads[0], gate_weight, up_weight, None, offsets, spans[0], rows, None, sums[1][:1]
        )
        (mine,) = hidden_grads(sums[1], gates, ups, spans[1], deps=[total, *in_blocks])
        grads.append((mine, swap_core(mine)))
    in_all = assemble(in_blocks, offsets if direct else in_order, deps=[mine])
    blocks = input_grads(
        *grads[-1], gate_weight, up_weight, total, offsets, spans[-1], rows, groups, [in_all]
    )

    def weight_part(before, i, span, deps):
        *weights, token = weight_grads(
            *grads[i], in_all, before, spans[i][0], span, units, deps
        )
        return weights, token

    cut = divisor(first, first // 2)
    weights, token = weight_part(None, 0, (0, cut), [])
    ready = blocks[0]
    if direct:
        far, third, kept, second, result = blocks
        far, third = swap_col(far, 1), swap_col(third, 2)
        sent6, sum4, sent1 = fold(
            [[(kept, 0), (far, 0)], [(kept, 1), (far, 1)], [(kept, 2), (third, 0)]],
            [False, True, False],
            deps=[token],
        )
        part6, part1 = swap_col(sent6, 2), swap_col(sent1, 1)
        ready = sent1
    if cut < first:
        weights, token = weight_part(weights, 0, (cut, first - cut), [ready])
    if direct:
        (sent4,) = fold([[(sum4, 0), (part6, 0)]], [False], deps=[token, part1])
        ready = sent4
    if len(spans) > 1:
        weights, token = weight_part(weights, 1, spans[1], [ready])
    if direct:
        result = result.astype(F32) + part1.astype(F32)
        for part in (swap_col(second, 2), swap_col(sent4, 4)):
            result = result + part.astype(F32)
        grad_inputs = result.astype(BF16)
    else:
        grad_inputs = lax.psum_scatter(blocks[0], "col", scatter_dimension=0, tiled=True)
    return grad_inputs, *weights, grad_down


def solution(mesh):
    return jax.shard_map(
        functools.partial(local, mesh.shape["row"], mesh.shape["col"]),
        mesh=mesh,
        in_specs=(
            P("col", "row"),
            P("col", "row"),
            P("row", "col"),
            P("row", "col"),
            P("row", "col"),
            P("row", "col"),
            P("col", "row"),
        ),
        out_specs=(P("col", "row"), P("row", "col"), P("row", "col"), P("col", "row")),
        check_vma=False,
    )
```

```python
import functools
import math

import jax
import jax.numpy as jnp
from jax import lax
from jax.experimental import pallas as pl
from jax.experimental.pallas import tpu as pltpu
from jax.sharding import PartitionSpec as P

F32 = jnp.float32
BF16 = jnp.bfloat16
CORES = 2
VMEM = 10 * 2**20
ANYWHERE = pl.BlockSpec(memory_space=pl.ANY)
REMAIN = pl.BlockSpec(memory_space=pltpu.HBM)
RESIDENT = pl.BlockSpec(memory_space=pltpu.VMEM)
SCALARS = pl.BlockSpec(memory_space=pltpu.SMEM)
WHOLE = pl.BlockSpec(memory_space=pltpu.VMEM)
NT = (((1,), (1,)), ((), ()))
TN = (((0,), (0,)), ((), ()))


def divisor(size, target, step=128):
    best = size
    for cand in range(step, target + 1, step):
        if size % cand == 0:
            best = cand
    return best


def call(kernel, operands, in_specs, out_shape, out_specs, deps=(), scratch=(), aliases=None, **kwargs):
    given = len(operands)
    total = given + len(deps)
    kept = {id(REMAIN): pltpu.HBM, id(RESIDENT): pltpu.VMEM}
    operands = [
        pltpu.with_memory_space_constraint(operand, kept[id(spec)]) if id(spec) in kept else operand
        for operand, spec in zip(operands, in_specs)
    ]

    held = sum(math.prod(s.shape) * s.dtype.itemsize for s in scratch if s.memory_space is pltpu.VMEM)

    def body(*refs):
        kernel(*refs[:given], *refs[total:])

    return pl.pallas_call(
        body,
        out_shape=out_shape,
        in_specs=list(in_specs) + [ANYWHERE] * len(deps),
        out_specs=out_specs,
        scratch_shapes=list(scratch),
        input_output_aliases=aliases or {},
        compiler_params=pltpu.CompilerParams(vmem_limit_bytes=VMEM + held),
        **kwargs,
    )(*operands, *deps)


def lay(blocks, offs, out, rows, first=0):
    i = first
    for block in blocks:
        for lo in range(0, block.shape[0], rows):
            out[pl.ds(pl.multiple_of(offs[i], rows), rows), :] = block[lo : lo + rows, :]
            i += 1


def assemble(blocks, offsets, deps=()):
    count, width = len(blocks), blocks[0].shape[1]
    tokens = sum(block.shape[0] for block in blocks)
    rows = tokens // offsets.shape[0]

    def kernel(offs, *refs):
        lay(refs[:count], offs, refs[count], rows)

    return call(
        kernel,
        [offsets, *blocks],
        [SCALARS] + [WHOLE] * count,
        jax.ShapeDtypeStruct((tokens, width), BF16),
        WHOLE,
        deps,
        name="assemble",
    )


def fetch(weight, span, others, deps=()):
    lo, units = span
    arrays = [weight, *others]
    shapes = [(units, weight.shape[1]), *(o.shape for o in others)]

    def kernel(*refs):
        given, outs, sems = refs[: len(arrays)], refs[len(arrays) : -1], refs[-1]
        copies = []
        for i, (source, out) in enumerate(zip(given, outs)):
            if i == 0:
                source = source.at[pl.ds(lo, units)]
            copies.append(pltpu.make_async_copy(source, out, sems.at[i]))
            copies[-1].start()
        for copy in copies:
            copy.wait()

    return call(
        kernel,
        arrays,
        [REMAIN] * len(arrays),
        [pltpu.VMEM(shape, BF16) for shape in shapes],
        [WHOLE] * len(arrays),
        deps,
        scratch=[pltpu.SemaphoreType.DMA((len(arrays),))],
        name="fetch",
    )


def run_copy(weight, lo, i, piece, ready, sems):
    at = pl.ds(pl.multiple_of(i * piece, piece), piece)
    return pltpu.make_async_copy(
        weight.at[pl.ds(pl.multiple_of(lo + i * piece, math.gcd(lo, piece)), piece)],
        ready.at[at],
        sems.at[i],
    )


def start_copies(weight, lo, count, piece, ready, sems):
    for i in range(count):
        run_copy(weight, lo, i, piece, ready, sems).start()


def dots_of(a, weight, lo, count, piece, ready, sems, keep, send):
    half = keep.shape[0]

    def step(i, carry):
        run_copy(weight, lo, i, piece, ready, sems).wait()
        at = pl.ds(pl.multiple_of(i * piece, piece), piece)
        part = lax.dot_general(a[...], ready[at, :], NT, preferred_element_type=F32).astype(BF16)
        keep[:, at] = part[:half]
        send[:, at] = part[half:]
        return carry

    lax.fori_loop(0, count, step, 0)


def first_partial(blocks, offsets, rows, deps=()):
    count, width = len(blocks), blocks[0].shape[1]
    tokens = sum(block.shape[0] for block in blocks)
    run = tokens // offsets.shape[0]
    half, units = tokens // CORES, rows.shape[0]
    piece = divisor(units, 640, 256)

    def kernel(offs, *refs):
        weight, keep, send, a = refs[count:]
        lay(refs[:count], offs, a, run)
        for lo in range(0, units, piece):
            at = slice(lo, lo + piece)
            part = lax.dot_general(a[...], weight[at, :], NT, preferred_element_type=F32)
            part = part.astype(BF16)
            keep[:, at] = part[:half]
            send[:, at] = part[half:]

    part = jax.ShapeDtypeStruct((half, units), BF16)
    return call(
        kernel,
        [offsets, *blocks, rows],
        [SCALARS] + [WHOLE] * count + [RESIDENT],
        (part, part, jax.ShapeDtypeStruct((tokens, width), BF16)),
        [WHOLE] * 3,
        deps,
        name="first_partial",
    )


def activations(gates, ups, deps=()):
    count = len(gates)
    rows, width = gates[0].shape

    def kernel(*refs):
        out = refs[2 * count]
        for i in range(count):
            gate = refs[i][...].astype(F32)
            up = refs[count + i][...].astype(F32)
            out[i * rows : (i + 1) * rows, :] = (gate * jax.nn.sigmoid(gate) * up).astype(BF16)

    return call(
        kernel,
        [*gates, *ups],
        [WHOLE] * (2 * count),
        jax.ShapeDtypeStruct((rows * count, width), BF16),
        WHOLE,
        deps,
        name="activations",
    )


def hidden_grads(sums, gates, ups, span, passed=(), deps=()):
    count = len(gates)
    rows = gates[0].shape[0]
    lo, units = span
    cols = slice(lo, lo + units)

    def kernel(*refs):
        out = refs[3 * count + len(passed)]
        for i in range(count):
            grad = 0.0
            for o in range(count):
                j = (i - o) % count
                grad = grad + refs[o][j * rows : (j + 1) * rows, :].astype(F32)
            gate = refs[count + i][:, cols].astype(F32)
            up = refs[2 * count + i][:, cols].astype(F32)
            sig = jax.nn.sigmoid(gate)
            at = slice(i * rows, (i + 1) * rows)
            out[0, at, :] = (grad * up * sig * (1.0 + gate * (1.0 - sig))).astype(BF16)
            out[1, at, :] = (grad * gate * sig).astype(BF16)

    shapes = [jax.ShapeDtypeStruct((2, rows * count, units), BF16)]
    shapes += [jax.ShapeDtypeStruct(p.shape, p.dtype) for p in passed]
    return call(
        kernel,
        [*sums, *gates, *ups, *passed],
        [WHOLE] * (3 * count) + [ANYWHERE] * len(passed),
        shapes,
        [WHOLE] + [ANYWHERE] * len(passed),
        deps,
        aliases={3 * count + i: 1 + i for i in range(len(passed))},
        name="hidden_grads",
    )


def both(mine, other, *at):
    return jnp.concatenate([mine[at], other[at]], axis=0)


def down_grad(hidden, hidden_other, out_all, down=None, span=(0, 0), deps=()):
    half, units = hidden.shape
    tokens, width = out_all.shape
    piece = divisor(units, 640)
    count = units // piece
    slots = min(3, count)
    lo, taken = span
    operands, specs = [hidden, hidden_other, out_all], [WHOLE] * 3
    shapes = [jax.ShapeDtypeStruct((units, width), BF16), jax.ShapeDtypeStruct((8, 128), F32)]
    scratch = [pltpu.VMEM((slots, piece, width), BF16), pltpu.SemaphoreType.DMA((slots,))]
    if taken:
        operands.append(down)
        specs.append(REMAIN)
        shapes += [jax.ShapeDtypeStruct((half, taken), BF16)] * 2
        run = divisor(taken, 1280)
        scratch += [pltpu.VMEM((taken, width), BF16), pltpu.SemaphoreType.DMA((taken // run,))]

    def kernel(*refs):
        a, b, g = refs[:3]
        given = len(operands)
        out, token = refs[given : given + 2]
        ready, sems = refs[given + len(shapes) : given + len(shapes) + 2]
        token[...] = jnp.zeros(token.shape, F32)
        if taken:
            start_copies(refs[3], lo, taken // run, run, refs[-2], refs[-1])

        def store(i):
            slot = lax.rem(i, slots)
            at = pl.ds(pl.multiple_of(i * piece, piece), piece)
            return pltpu.make_async_copy(ready.at[slot], out.at[at], sems.at[slot])

        def step(i, carry):
            @pl.when(i >= slots)
            def _():
                store(i - slots).wait()

            at = pl.ds(pl.multiple_of(i * piece, piece), piece)
            ready[lax.rem(i, slots)] = lax.dot_general(
                both(a, b, slice(None), at), g[...], TN, preferred_element_type=F32
            ).astype(BF16)
            store(i).start()
            return carry

        lax.fori_loop(0, count, step, 0)
        if taken:
            dots_of(
                g, refs[3], lo, taken // run, run, refs[-2], refs[-1], refs[given + 2], refs[given + 3]
            )
        for i in range(count - slots, count):
            store(i).wait()

    return call(
        kernel,
        operands,
        specs,
        shapes,
        [REMAIN] + [WHOLE] * (len(shapes) - 1),
        deps,
        scratch=scratch,
        name="down_grad",
    )


def input_grads(mine, other, gate_weight, up_weight, before, offsets, span, rows, groups, deps=()):
    _, half, units = mine.shape
    tokens = 2 * half
    width = gate_weight.shape[0]
    piece = divisor(width, 512)
    pieces = width // piece
    slots = min(4, pieces)
    cols = slice(span[0], span[0] + units)
    operands = [offsets, mine, other, gate_weight, up_weight] + ([] if before is None else [before])
    specs = [SCALARS, WHOLE, WHOLE, REMAIN, REMAIN] + ([] if before is None else [WHOLE])
    if groups is None:
        shapes = [jax.ShapeDtypeStruct((tokens, width), F32)]
    else:
        shapes = [jax.ShapeDtypeStruct((rows * len(group), width), BF16) for group in groups]

    def kernel(*refs):
        offs, a, b, gw, uw = refs[:5]
        outs = refs[len(operands) : len(operands) + len(shapes)]
        sums, ready, sems = refs[-3:]
        copies = []
        for j in range(pieces):
            at = slice(j * piece, (j + 1) * piece)
            for i, w in enumerate((gw, uw)):
                copies.append(
                    pltpu.make_async_copy(
                        w.at[at, cols], ready.at[i, j % slots], sems.at[i, j % slots]
                    )
                )
        for copy in copies[: 2 * slots]:
            copy.start()
        for j in range(pieces):
            at = slice(j * piece, (j + 1) * piece)
            total = 0.0 if before is None else refs[5][:, at]
            for i in range(2):
                copies[2 * j + i].wait()
            for i in range(2):
                total = total + lax.dot_general(
                    both(a, b, i), ready[i, j % slots], NT, preferred_element_type=F32
                )
            sums[:, at] = total
            for copy in copies[2 * (j + slots) : 2 * (j + slots + 1)]:
                copy.start()
        if groups is None:
            outs[0][...] = sums[...]
        for out, group in zip(outs, groups or ()):
            for i, m in enumerate(group):
                at = pl.ds(pl.multiple_of(offs[m], rows), rows)
                out[i * rows : (i + 1) * rows, :] = sums[at, :].astype(BF16)

    return call(
        kernel,
        operands,
        specs,
        shapes,
        [WHOLE] * len(shapes),
        deps,
        scratch=[
            pltpu.VMEM((tokens, width), F32),
            pltpu.VMEM((2, slots, piece, units), BF16),
            pltpu.SemaphoreType.DMA((2, slots)),
        ],
        name="input_grads",
    )


def fold(terms, wide, rows, deps=()):
    arrays, refs_of = [], []
    for term in terms:
        refs_of.append([])
        for array, row in term:
            known = [i for i, a in enumerate(arrays) if a is array]
            if not known:
                arrays.append(array)
            refs_of[-1].append((known[0] if known else len(arrays) - 1, row))
    width = arrays[0].shape[1]
    kinds = [F32 if w else BF16 for w in wide]

    def kernel(*refs):
        for out, pairs in zip(refs[len(arrays) :], refs_of):
            total = 0.0
            for i, row in pairs:
                total = total + refs[i][row * rows : (row + 1) * rows, :].astype(F32)
            out[...] = total.astype(out.dtype)

    return call(
        kernel,
        arrays,
        [WHOLE] * len(arrays),
        [jax.ShapeDtypeStruct((rows, width), kind) for kind in kinds],
        [WHOLE] * len(terms),
        deps,
        name="fold",
    )


def weight_grads(mine, other, in_all, before, start, span, whole, deps=()):
    skip, units = span[0] - start, span[1]
    tokens, width = in_all.shape
    piece = divisor(width, 256)
    count = width // piece
    slots = min(8, count)
    cols = slice(span[0], span[0] + units)

    def kernel(*refs):
        a, b, x = refs[:3]
        outs, token, ready, sems = refs[-5:-3], refs[-3], refs[-2], refs[-1]
        token[...] = jnp.zeros(token.shape, F32)
        taken = slice(skip, skip + units)
        copies = []
        for j in range(count):
            at, slot = slice(j * piece, (j + 1) * piece), j % slots
            for i in range(2):
                if j >= slots:
                    copies[2 * (j - slots) + i].wait()
                ready[i, slot] = lax.dot_general(
                    x[:, at], both(a, b, i, slice(None), taken), TN, preferred_element_type=F32
                ).astype(BF16)
                copy = pltpu.make_async_copy(
                    ready.at[i, slot], outs[i].at[at, cols], sems.at[i, slot]
                )
                copy.start()
                copies.append(copy)
        for copy in copies[2 * (count - slots) :]:
            copy.wait()

    shape = jax.ShapeDtypeStruct((width, whole), BF16)
    return call(
        kernel,
        [mine, other, in_all, *(before or ())],
        [WHOLE] * 3 + [REMAIN] * (2 if before else 0),
        (shape, shape, jax.ShapeDtypeStruct((8, 128), F32)),
        [REMAIN, REMAIN, WHOLE],
        deps,
        scratch=[
            pltpu.VMEM((2, slots, piece, units), BF16),
            pltpu.SemaphoreType.DMA((2, slots)),
        ],
        aliases={3: 0, 4: 1} if before else None,
        name="weight_grads",
    )


def local(nr, nc, inputs, grad_out, gate, up, gate_weight, up_weight, down_weight):
    nx = nr // CORES
    row, col = lax.axis_index("row"), lax.axis_index("col")
    x, core = row // CORES, row % CORES
    own_tokens = gate.shape[0]
    col_tokens = grad_out.shape[0]
    units = down_weight.shape[0]
    first = units // 5 * 3 if units % 640 == 0 else units
    spans = [(0, first)] + ([(first, units - first)] if first < units else [])
    direct = nc == 8 and nr * own_tokens == nc * col_tokens and own_tokens % col_tokens == 0

    def swap_core(value):
        return lax.ppermute(value, "row", [(r, r ^ 1) for r in range(nr)])

    def from_x(value, offset):
        return lax.ppermute(value, "row", [((r + offset * CORES) % nr, r) for r in range(nr)])

    def swap_col(value, mask):
        return lax.ppermute(value, "col", [(c, c ^ mask) for c in range(nc)])

    def place(block):
        block_x, block_core = block // CORES, block % CORES
        return ((block_core ^ core) * nx + (block_x - x + nx) % nx) * own_tokens

    in_order = jnp.stack([place(r) for r in range(nr)]).astype(jnp.int32)
    if direct:
        rows, per = col_tokens, own_tokens // col_tokens
        places = [place((col ^ m) // per) + ((col ^ m) % per) * rows for m in range(nc)]
        offsets = jnp.stack(places).astype(jnp.int32)
    else:
        rows, offsets = own_tokens, in_order

    def gather(value):
        if not direct:
            return [lax.all_gather(value, "col", axis=0, tiled=True)]
        got = {0: value}
        got[1] = swap_col(value, 1)
        got[4] = swap_col(value, 4)
        got[2] = swap_col(value, 2)
        got[3] = swap_col(got[1], 2)
        got[6] = swap_col(got[4], 2)
        got[5] = swap_col(got[4], 1)
        got[7] = swap_col(got[6], 1)
        return [got[m] for m in range(nc)]

    gates = [gate] + [from_x(gate, o) for o in range(1, nx)]
    ups = [up] + [from_x(up, o) for o in range(1, nx)]

    def exchanged(keep, send):
        total = (keep.astype(F32) + swap_core(send).astype(F32)).astype(BF16)
        return [total] + [from_x(total, o) for o in range(1, nx)]

    blocks = gather(grad_out)
    late = blocks[6:7]
    if direct:
        rows_here, blocks[0], gates[0], ups[0] = fetch(
            down_weight, spans[0], [grad_out, gate, up], deps=late
        )
    else:
        rows_here, gates[0], ups[0] = fetch(down_weight, spans[0], [gate, up])
    beside = [swap_col(inputs, 1)] if direct else []
    keep, send, out_all = first_partial(
        blocks, offsets, rows_here, deps=[*gates[1:], *ups[1:], *beside]
    )
    hidden = activations(gates, ups, deps=[keep])
    hidden_other = swap_core(hidden)
    sums = [exchanged(keep, send)]
    if direct:
        own = jnp.concatenate([inputs, *beside], axis=0)
        in_blocks = [own, swap_col(own, 2), swap_col(own, 4)]
    else:
        own = sums[0][0]
        in_blocks = [lax.all_gather(inputs, "col", axis=0, tiled=True)]
    span = spans[1] if len(spans) > 1 else (0, 0)
    grad_down, token, *parts = down_grad(
        hidden, hidden_other, out_all, down_weight, span, deps=[sums[0][0], own]
    )

    mine, *parts = hidden_grads(sums[0], gates, ups, spans[0], parts, [token, *in_blocks])
    grads = [(mine, swap_core(mine))]
    groups = [(7, 5), (3, 2), (6, 4, 1), (0,)] if direct else [range(nr)]
    if direct:
        in_blocks.append(swap_col(in_blocks[2], 2))
    total = None
    if len(spans) > 1:
        sums.append(exchanged(*parts))
        (total,) = input_grads(
            *grads[0], gate_weight, up_weight, None, offsets, spans[0], rows, None, sums[1][:1]
        )
        (mine,) = hidden_grads(sums[1], gates, ups, spans[1], deps=[total, *in_blocks])
        grads.append((mine, swap_core(mine)))
    in_all = assemble(in_blocks, offsets if direct else in_order, deps=[mine])
    blocks = input_grads(
        *grads[-1], gate_weight, up_weight, total, offsets, spans[-1], rows, groups, [in_all]
    )

    def weight_part(before, i, span, deps):
        *weights, token = weight_grads(
            *grads[i], in_all, before, spans[i][0], span, units, deps
        )
        return weights, token

    cut = divisor(first, first // 2)
    parts = [(0, (0, cut)), (0, (cut, first - cut))]
    parts = parts[: 1 if cut == first else 2]
    if len(spans) > 1:
        parts.insert(0, (1, spans[1]))
    weights, token = weight_part(None, *parts[0], [])
    ready = blocks[0]
    if direct:
        far, near, kept, result = blocks
        far, near = swap_col(far, 1), swap_col(near, 2)
        sent6, sum4 = fold(
            [[(kept, 0), (far, 0)], [(kept, 1), (far, 1)]], [False, True], rows, deps=[token]
        )
        part6 = swap_col(sent6, 2)
        ready = sent6
    if len(parts) > 1:
        weights, token = weight_part(weights, *parts[1], [ready])
    if direct:
        sent4, sent1 = fold(
            [[(sum4, 0), (part6, 0)], [(kept, 2), (near, 0)]], [False, False], rows, deps=[token]
        )
        ready = sent4
    if len(parts) > 2:
        weights, token = weight_part(weights, *parts[2], [ready])
    if direct:
        result = result.astype(F32) + near[rows:].astype(F32) + swap_col(sent1, 1).astype(F32)
        result = result + swap_col(sent4, 4).astype(F32)
        grad_inputs = result.astype(BF16)
    else:
        grad_inputs = lax.psum_scatter(blocks[0], "col", scatter_dimension=0, tiled=True)
    return grad_inputs, *weights, grad_down


def solution(mesh):
    return jax.shard_map(
        functools.partial(local, mesh.shape["row"], mesh.shape["col"]),
        mesh=mesh,
        in_specs=(
            P("col", "row"),
            P("col", "row"),
            P("row", "col"),
            P("row", "col"),
            P("row", "col"),
            P("row", "col"),
            P("col", "row"),
        ),
        out_specs=(P("col", "row"), P("row", "col"), P("row", "col"), P("col", "row")),
        check_vma=False,
    )
```

```python
import functools
import math

import jax
import jax.numpy as jnp
from jax import lax
from jax.experimental import pallas as pl
from jax.experimental.pallas import tpu as pltpu
from jax.sharding import PartitionSpec as P

F32 = jnp.float32
BF16 = jnp.bfloat16
CORES = 2
VMEM = 10 * 2**20
ANYWHERE = pl.BlockSpec(memory_space=pl.ANY)
REMAIN = pl.BlockSpec(memory_space=pltpu.HBM)
RESIDENT = pl.BlockSpec(memory_space=pltpu.VMEM)
SCALARS = pl.BlockSpec(memory_space=pltpu.SMEM)
WHOLE = pl.BlockSpec(memory_space=pltpu.VMEM)
NT = (((1,), (1,)), ((), ()))
TN = (((0,), (0,)), ((), ()))


def divisor(size, target, step=128):
    best = size
    for cand in range(step, target + 1, step):
        if size % cand == 0:
            best = cand
    return best


def call(kernel, operands, in_specs, out_shape, out_specs, deps=(), scratch=(), aliases=None, **kwargs):
    given = len(operands)
    total = given + len(deps)
    kept = {id(REMAIN): pltpu.HBM, id(RESIDENT): pltpu.VMEM}
    operands = [
        pltpu.with_memory_space_constraint(operand, kept[id(spec)]) if id(spec) in kept else operand
        for operand, spec in zip(operands, in_specs)
    ]

    held = sum(math.prod(s.shape) * s.dtype.itemsize for s in scratch if s.memory_space is pltpu.VMEM)

    def body(*refs):
        kernel(*refs[:given], *refs[total:])

    return pl.pallas_call(
        body,
        out_shape=out_shape,
        in_specs=list(in_specs) + [ANYWHERE] * len(deps),
        out_specs=out_specs,
        scratch_shapes=list(scratch),
        input_output_aliases=aliases or {},
        compiler_params=pltpu.CompilerParams(vmem_limit_bytes=VMEM + held),
        **kwargs,
    )(*operands, *deps)


def lay(blocks, offs, out, rows, first=0):
    i = first
    for block in blocks:
        for lo in range(0, block.shape[0], rows):
            out[pl.ds(pl.multiple_of(offs[i], rows), rows), :] = block[lo : lo + rows, :]
            i += 1


def assemble(blocks, offsets, deps=()):
    count, width = len(blocks), blocks[0].shape[1]
    tokens = sum(block.shape[0] for block in blocks)
    rows = tokens // offsets.shape[0]

    def kernel(offs, *refs):
        lay(refs[:count], offs, refs[count], rows)

    return call(
        kernel,
        [offsets, *blocks],
        [SCALARS] + [WHOLE] * count,
        jax.ShapeDtypeStruct((tokens, width), BF16),
        WHOLE,
        deps,
        name="assemble",
    )


def fetch(weight, span, others, deps=()):
    lo, units = span
    arrays = [weight, *others]
    shapes = [(units, weight.shape[1]), *(o.shape for o in others)]

    def kernel(*refs):
        given, outs, sems = refs[: len(arrays)], refs[len(arrays) : -1], refs[-1]
        copies = []
        for i, (source, out) in enumerate(zip(given, outs)):
            if i == 0:
                source = source.at[pl.ds(lo, units)]
            copies.append(pltpu.make_async_copy(source, out, sems.at[i]))
            copies[-1].start()
        for copy in copies:
            copy.wait()

    return call(
        kernel,
        arrays,
        [REMAIN] * len(arrays),
        [pltpu.VMEM(shape, BF16) for shape in shapes],
        [WHOLE] * len(arrays),
        deps,
        scratch=[pltpu.SemaphoreType.DMA((len(arrays),))],
        name="fetch",
    )


def run_copy(weight, lo, i, piece, ready, sems):
    at = pl.ds(pl.multiple_of(i * piece, piece), piece)
    return pltpu.make_async_copy(
        weight.at[pl.ds(pl.multiple_of(lo + i * piece, math.gcd(lo, piece)), piece)],
        ready.at[at],
        sems.at[i],
    )


def start_copies(weight, lo, count, piece, ready, sems):
    for i in range(count):
        run_copy(weight, lo, i, piece, ready, sems).start()


def dots_of(a, weight, lo, count, piece, ready, sems, keep, send):
    half = keep.shape[0]

    def step(i, carry):
        run_copy(weight, lo, i, piece, ready, sems).wait()
        at = pl.ds(pl.multiple_of(i * piece, piece), piece)
        part = lax.dot_general(a[...], ready[at, :], NT, preferred_element_type=F32).astype(BF16)
        keep[:, at] = part[:half]
        send[:, at] = part[half:]
        return carry

    lax.fori_loop(0, count, step, 0)


def first_partial(blocks, offsets, rows, deps=()):
    count, width = len(blocks), blocks[0].shape[1]
    tokens = sum(block.shape[0] for block in blocks)
    run = tokens // offsets.shape[0]
    half, units = tokens // CORES, rows.shape[0]
    piece = min(units, 256)

    def kernel(offs, *refs):
        weight, keep, send, a = refs[count:]
        lay(refs[:count], offs, a, run)
        for lo in range(0, units, piece):
            at = slice(lo, min(lo + piece, units))
            part = lax.dot_general(a[...], weight[at, :], NT, preferred_element_type=F32)
            part = part.astype(BF16)
            keep[:, at] = part[:half]
            send[:, at] = part[half:]

    part = jax.ShapeDtypeStruct((half, units), BF16)
    return call(
        kernel,
        [offsets, *blocks, rows],
        [SCALARS] + [WHOLE] * count + [RESIDENT],
        (part, part, jax.ShapeDtypeStruct((tokens, width), BF16)),
        [WHOLE] * 3,
        deps,
        name="first_partial",
    )


def activations(gates, ups, deps=()):
    count = len(gates)
    rows, width = gates[0].shape

    def kernel(*refs):
        out = refs[2 * count]
        for i in range(count):
            gate = refs[i][...].astype(F32)
            up = refs[count + i][...].astype(F32)
            out[i * rows : (i + 1) * rows, :] = (gate * jax.nn.sigmoid(gate) * up).astype(BF16)

    return call(
        kernel,
        [*gates, *ups],
        [WHOLE] * (2 * count),
        jax.ShapeDtypeStruct((rows * count, width), BF16),
        WHOLE,
        deps,
        name="activations",
    )


def hidden_grads(sums, gates, ups, span, deps=()):
    count = len(gates)
    rows = gates[0].shape[0]
    lo, units = span
    cols = slice(lo, lo + units)

    def kernel(*refs):
        out = refs[3 * count]
        for i in range(count):
            grad = 0.0
            for o in range(count):
                j = (i - o) % count
                grad = grad + refs[o][j * rows : (j + 1) * rows, :].astype(F32)
            gate = refs[count + i][:, cols].astype(F32)
            up = refs[2 * count + i][:, cols].astype(F32)
            sig = jax.nn.sigmoid(gate)
            at = slice(i * rows, (i + 1) * rows)
            out[0, at, :] = (grad * up * sig * (1.0 + gate * (1.0 - sig))).astype(BF16)
            out[1, at, :] = (grad * gate * sig).astype(BF16)

    return call(
        kernel,
        [*sums, *gates, *ups],
        [WHOLE] * (3 * count),
        jax.ShapeDtypeStruct((2, rows * count, units), BF16),
        WHOLE,
        deps,
        name="hidden_grads",
    )


def hand_over(arrays, deps):
    def kernel(*refs):
        del refs

    return call(
        kernel,
        arrays,
        [ANYWHERE] * len(arrays),
        [jax.ShapeDtypeStruct(a.shape, a.dtype) for a in arrays],
        [ANYWHERE] * len(arrays),
        deps,
        aliases={i: i for i in range(len(arrays))},
        name="hand_over",
    )


def both(mine, other, *at):
    return jnp.concatenate([mine[at], other[at]], axis=0)


def down_grad(
    hidden, hidden_other, out_all, down=None, span=(0, 0), coming=(), coming_span=(0, 0), head=0, deps=()
):
    half, units = hidden.shape
    tokens, width = out_all.shape
    piece = divisor(units, 640)
    count = units // piece
    slots = min(3, count)
    lo, taken = span
    operands, specs = [hidden, hidden_other, out_all], [WHOLE] * 3
    shapes = [jax.ShapeDtypeStruct((units, width), BF16), jax.ShapeDtypeStruct((8, 128), F32)]
    scratch = [pltpu.VMEM((slots, piece, width), BF16), pltpu.SemaphoreType.DMA((slots,))]
    if taken:
        operands.append(down)
        specs.append(REMAIN)
        shapes += [jax.ShapeDtypeStruct((half, taken), BF16)] * 2
        run = divisor(taken, 1536)
        operands += coming
        specs += [REMAIN] * len(coming)
        shapes += [pltpu.VMEM((head, coming_span[1]), BF16)] * len(coming)
        scratch += [
            pltpu.VMEM((taken, width), BF16),
            pltpu.SemaphoreType.DMA((taken // run + len(coming),)),
        ]

    def kernel(*refs):
        a, b, g = refs[:3]
        given = len(operands)
        out, token = refs[given : given + 2]
        ready, sems = refs[given + len(shapes) : given + len(shapes) + 2]
        token[...] = jnp.zeros(token.shape, F32)
        if taken:
            start_copies(refs[3], lo, taken // run, run, refs[-2], refs[-1])
            loads = []
            for i in range(len(coming)):
                source = refs[4 + i].at[pl.ds(0, head), pl.ds(*coming_span)]
                sem = refs[-1].at[taken // run + i]
                loads.append(pltpu.make_async_copy(source, refs[given + 4 + i], sem))
                loads[-1].start()

        def store(i):
            slot = lax.rem(i, slots)
            at = pl.ds(pl.multiple_of(i * piece, piece), piece)
            return pltpu.make_async_copy(ready.at[slot], out.at[at], sems.at[slot])

        def step(i, carry):
            @pl.when(i >= slots)
            def _():
                store(i - slots).wait()

            at = pl.ds(pl.multiple_of(i * piece, piece), piece)
            ready[lax.rem(i, slots)] = lax.dot_general(
                both(a, b, slice(None), at), g[...], TN, preferred_element_type=F32
            ).astype(BF16)
            store(i).start()
            return carry

        lax.fori_loop(0, count, step, 0)
        if taken:
            dots_of(
                g, refs[3], lo, taken // run, run, refs[-2], refs[-1], refs[given + 2], refs[given + 3]
            )
            for load in loads:
                load.wait()
        for i in range(count - slots, count):
            store(i).wait()

    return call(
        kernel,
        operands,
        specs,
        shapes,
        [REMAIN] + [WHOLE] * (len(shapes) - 1),
        deps,
        scratch=scratch,
        name="down_grad",
    )


def input_grads(
    mine, other, gate_weight, up_weight, before, offsets, span, rows, groups, heads=(), deps=()
):
    _, half, units = mine.shape
    tokens = 2 * half
    width = gate_weight.shape[0]
    piece = divisor(width, 512)
    pieces = width // piece
    cols = slice(span[0], span[0] + units)
    skip = heads[0].shape[0] // piece if heads else 0
    operands = [offsets, mine, other, gate_weight, up_weight, *heads]
    operands += [] if before is None else [before]
    specs = [SCALARS, WHOLE, WHOLE, REMAIN, REMAIN] + [RESIDENT] * len(heads)
    specs += [] if before is None else [WHOLE]
    if groups is None:
        shapes = [jax.ShapeDtypeStruct((tokens, width), F32)]
    else:
        shapes = [jax.ShapeDtypeStruct((rows * len(group), width), BF16) for group in groups]

    def kernel(*refs):
        offs, a, b, gw, uw = refs[:5]
        outs = refs[len(operands) : len(operands) + len(shapes)]
        sums, ready, sems = refs[-3:]
        copies = []
        for j in range(skip, pieces):
            at = slice(j * piece, (j + 1) * piece)
            for i, w in enumerate((gw, uw)):
                copies.append(
                    pltpu.make_async_copy(w.at[at, cols], ready.at[i, j - skip], sems.at[i, j - skip])
                )
                copies[-1].start()
        for j in range(pieces):
            at = slice(j * piece, (j + 1) * piece)
            total = 0.0 if before is None else refs[len(operands) - 1][:, at]
            if j >= skip:
                for i in range(2):
                    copies[2 * (j - skip) + i].wait()
            for i in range(2):
                w = refs[5 + i][at, :] if j < skip else ready[i, j - skip]
                total = total + lax.dot_general(both(a, b, i), w, NT, preferred_element_type=F32)
            sums[:, at] = total
        if groups is None:
            outs[0][...] = sums[...]
        for out, group in zip(outs, groups or ()):
            for i, m in enumerate(group):
                at = pl.ds(pl.multiple_of(offs[m], rows), rows)
                out[i * rows : (i + 1) * rows, :] = sums[at, :].astype(BF16)

    return call(
        kernel,
        operands,
        specs,
        shapes,
        [WHOLE] * len(shapes),
        deps,
        scratch=[
            pltpu.VMEM((tokens, width), F32),
            pltpu.VMEM((2, pieces - skip, piece, units), BF16),
            pltpu.SemaphoreType.DMA((2, pieces - skip)),
        ],
        name="input_grads",
    )


def fold(terms, wide, rows, deps=()):
    arrays, refs_of = [], []
    for term in terms:
        refs_of.append([])
        for array, row in term:
            known = [i for i, a in enumerate(arrays) if a is array]
            if not known:
                arrays.append(array)
            refs_of[-1].append((known[0] if known else len(arrays) - 1, row))
    width = arrays[0].shape[1]
    kinds = [F32 if w else BF16 for w in wide]

    def kernel(*refs):
        for out, pairs in zip(refs[len(arrays) :], refs_of):
            total = 0.0
            for i, row in pairs:
                total = total + refs[i][row * rows : (row + 1) * rows, :].astype(F32)
            out[...] = total.astype(out.dtype)

    return call(
        kernel,
        arrays,
        [WHOLE] * len(arrays),
        [jax.ShapeDtypeStruct((rows, width), kind) for kind in kinds],
        [WHOLE] * len(terms),
        deps,
        name="fold",
    )


def weight_grads(mine, other, in_all, before, start, span, whole, deps=()):
    skip, units = span[0] - start, span[1]
    tokens, width = in_all.shape
    piece = divisor(width, 256)
    count = width // piece
    slots = min(8, count)
    cols = slice(span[0], span[0] + units)

    def kernel(*refs):
        a, b, x = refs[:3]
        outs, token, ready, sems = refs[-5:-3], refs[-3], refs[-2], refs[-1]
        token[...] = jnp.zeros(token.shape, F32)
        taken = slice(skip, skip + units)
        copies = []
        for j in range(count):
            at, slot = slice(j * piece, (j + 1) * piece), j % slots
            for i in range(2):
                if j >= slots:
                    copies[2 * (j - slots) + i].wait()
                ready[i, slot] = lax.dot_general(
                    x[:, at], both(a, b, i, slice(None), taken), TN, preferred_element_type=F32
                ).astype(BF16)
                copy = pltpu.make_async_copy(
                    ready.at[i, slot], outs[i].at[at, cols], sems.at[i, slot]
                )
                copy.start()
                copies.append(copy)
        for copy in copies[2 * (count - slots) :]:
            copy.wait()

    shape = jax.ShapeDtypeStruct((width, whole), BF16)
    return call(
        kernel,
        [mine, other, in_all, *(before or ())],
        [WHOLE] * 3 + [REMAIN] * (2 if before else 0),
        (shape, shape, jax.ShapeDtypeStruct((8, 128), F32)),
        [REMAIN, REMAIN, WHOLE],
        deps,
        scratch=[
            pltpu.VMEM((2, slots, piece, units), BF16),
            pltpu.SemaphoreType.DMA((2, slots)),
        ],
        aliases={3: 0, 4: 1} if before else None,
        name="weight_grads",
    )


def local(nr, nc, inputs, grad_out, gate, up, gate_weight, up_weight, down_weight):
    nx = nr // CORES
    row, col = lax.axis_index("row"), lax.axis_index("col")
    x, core = row // CORES, row % CORES
    own_tokens = gate.shape[0]
    col_tokens = grad_out.shape[0]
    units = down_weight.shape[0]
    first = units // 30 * 19 if units % 3840 == 0 else units
    spans = [(0, first)] + ([(first, units - first)] if first < units else [])
    direct = nc == 8 and nr * own_tokens == nc * col_tokens and own_tokens % col_tokens == 0

    def swap_core(value):
        return lax.ppermute(value, "row", [(r, r ^ 1) for r in range(nr)])

    def from_x(value, offset):
        return lax.ppermute(value, "row", [((r + offset * CORES) % nr, r) for r in range(nr)])

    def swap_col(value, mask):
        return lax.ppermute(value, "col", [(c, c ^ mask) for c in range(nc)])

    def place(block):
        block_x, block_core = block // CORES, block % CORES
        return ((block_core ^ core) * nx + (block_x - x + nx) % nx) * own_tokens

    in_order = jnp.stack([place(r) for r in range(nr)]).astype(jnp.int32)
    if direct:
        rows, per = col_tokens, own_tokens // col_tokens
        places = [place((col ^ m) // per) + ((col ^ m) % per) * rows for m in range(nc)]
        offsets = jnp.stack(places).astype(jnp.int32)
    else:
        rows, offsets = own_tokens, in_order

    def gather(value):
        if not direct:
            return [lax.all_gather(value, "col", axis=0, tiled=True)]
        got = {0: value}
        got[1] = swap_col(value, 1)
        got[4] = swap_col(value, 4)
        got[2] = swap_col(value, 2)
        got[3] = swap_col(got[1], 2)
        got[6] = swap_col(got[4], 2)
        got[5] = swap_col(got[4], 1)
        got[7] = swap_col(got[6], 1)
        return [got[m] for m in range(nc)]

    gates = [gate] + [from_x(gate, o) for o in range(1, nx)]
    ups = [up] + [from_x(up, o) for o in range(1, nx)]

    def exchanged(keep, send):
        total = (keep.astype(F32) + swap_core(send).astype(F32)).astype(BF16)
        return [total] + [from_x(total, o) for o in range(1, nx)]

    blocks = gather(grad_out)
    late = blocks[6:7]
    if direct:
        rows_here, blocks[0], gates[0], ups[0] = fetch(
            down_weight, spans[0], [grad_out, gate, up], deps=late
        )
    else:
        rows_here, gates[0], ups[0] = fetch(down_weight, spans[0], [gate, up])
    beside = [swap_col(inputs, 1)] if direct else []
    keep, send, out_all = first_partial(
        blocks, offsets, rows_here, deps=[*gates[1:], *ups[1:], *beside]
    )
    hidden = activations(gates, ups, deps=[keep])
    hidden_other = swap_core(hidden)
    sums = [exchanged(keep, send)]
    if direct:
        own = jnp.concatenate([inputs, *beside], axis=0)
        in_blocks = [own, swap_col(own, 2), swap_col(own, 4)]
    else:
        own = sums[0][0]
        in_blocks = [lax.all_gather(inputs, "col", axis=0, tiled=True)]
    span = spans[1] if len(spans) > 1 else (0, 0)
    grad_down, token, *parts = down_grad(
        hidden,
        hidden_other,
        out_all,
        down_weight,
        span,
        [gate_weight, up_weight],
        spans[0],
        divisor(gate_weight.shape[0], 512),
        deps=[sums[0][0], own],
    )
    parts, heads = parts[:2], parts[2:]

    first_deps = [token, *sums[0][1:], *in_blocks, *heads]
    if len(spans) > 1:
        sums.append(exchanged(*hand_over(parts, first_deps)))
        first_deps = sums[1][:1]
    mine = hidden_grads(sums[0], gates, ups, spans[0], first_deps)
    grads = [(mine, swap_core(mine))]
    groups = [(7, 5), (3, 2), (6, 4, 1), (0,)] if direct else [range(nr)]
    if direct:
        in_blocks.append(swap_col(in_blocks[2], 2))
    total = None
    if len(spans) > 1:
        (total,) = input_grads(
            *grads[0], gate_weight, up_weight, None, offsets, spans[0], rows, None,
            heads, sums[1][:1],
        )
        mine = hidden_grads(sums[1], gates, ups, spans[1], deps=[total, *in_blocks])
        grads.append((mine, swap_core(mine)))
    in_all = assemble(in_blocks, offsets if direct else in_order, deps=[mine])
    blocks = input_grads(
        *grads[-1], gate_weight, up_weight, total, offsets, spans[-1], rows, groups, (), [in_all]
    )

    def weight_part(before, i, span, deps):
        *weights, token = weight_grads(
            *grads[i], in_all, before, spans[i][0], span, units, deps
        )
        return weights, token

    cut = (first // 256 - 1) * 128 if first % 128 == 0 and first >= 512 else first
    parts = [(0, (0, cut)), (0, (cut, first - cut))]
    parts = parts[: 1 if cut == first else 2]
    if len(spans) > 1:
        parts.insert(0, (1, spans[1]))
    weights, token = weight_part(None, *parts[0], [])
    ready = blocks[0]
    if direct:
        far, near, kept, result = blocks
        far, near = swap_col(far, 1), swap_col(near, 2)
        sent6, sum4 = fold(
            [[(kept, 0), (far, 0)], [(kept, 1), (far, 1)]], [False, True], rows, deps=[token]
        )
        part6 = swap_col(sent6, 2)
        ready = sent6
    if len(parts) > 1:
        weights, token = weight_part(weights, *parts[1], [ready])
    if direct:
        sent4, sent1 = fold(
            [[(sum4, 0), (part6, 0)], [(kept, 2), (near, 0)]], [False, False], rows, deps=[token]
        )
        ready = sent4
    if len(parts) > 2:
        weights, token = weight_part(weights, *parts[2], [ready])
    if direct:
        result = result.astype(F32) + near[rows:].astype(F32) + swap_col(sent1, 1).astype(F32)
        result = result + swap_col(sent4, 4).astype(F32)
        grad_inputs = result.astype(BF16)
    else:
        grad_inputs = lax.psum_scatter(blocks[0], "col", scatter_dimension=0, tiled=True)
    return grad_inputs, *weights, grad_down


def solution(mesh):
    return jax.shard_map(
        functools.partial(local, mesh.shape["row"], mesh.shape["col"]),
        mesh=mesh,
        in_specs=(
            P("col", "row"),
            P("col", "row"),
            P("row", "col"),
            P("row", "col"),
            P("row", "col"),
            P("row", "col"),
            P("col", "row"),
        ),
        out_specs=(P("col", "row"), P("row", "col"), P("row", "col"), P("col", "row")),
        check_vma=False,
    )
```
